256 devices in a mesh: seq: 16 (over z, core), ch: 4 (over x), dp: 4 (over y).
Axes of the slice: x: 4, y: 4, z: 8, core: 2. Of those that a mesh axis runs over, the one named last changes fastest.
Arguments:
- grad_out: bfloat16 [4, 2048, 4096], P('dp', 'seq', 'ch'), may hold values from -6 to 6
- inputs: bfloat16 [4, 2048, 4096], P('dp', 'seq', 'ch'), may hold values from -6 to 6
- decay_rate: float32 [64, 4096], P(None, 'ch'), may hold values from 0.01 to 103
- frequency: float32 [64, 4096], P(None, 'ch'), may hold values from -3.140625 to 3.140625
- in_proj: float32 [2, 64, 4096], P(None, None, 'ch'), may hold values from -6 to 6
- out_proj: float32 [2, 64, 4096], P(None, None, 'ch'), may hold values from -0.015625 to 0.015625
- skip_gain: float32 [4096], P('ch'), may hold values from 0.1 to 1.9
- doc_lengths: int32 [4, 4], P('dp'), may hold values from 1 to 1024, 2048 in all within a row
- piece_lengths: int32 [4, 16, 4], P('dp', 'seq'), may hold values from 1 to 64, 128 in all within a row
Outputs:
- returned: bfloat16 [16, 4, 4, 64, 4096], P('seq', 'dp', None, None, 'ch')
- grad_b: float32 [2, 64, 4096], P(None, None, 'ch')
The draws below stay inside these ranges and needn't reach their ends.
Inputs may be any that keep to these rules, and one draw needn't show every extreme that they name: `doc_lengths`: the lengths of a row sum to 2048, and the largest is exactly 1024. `piece_lengths`: the lengths of one row and index of seq sum to 128, and the largest is exactly 64.
All inputs are finite; a program needn't handle non-finite values.
Results may differ from the reference program's by a relative error of at most 0.0013.
Values may be sent and summed in bfloat16 or wider, within the bound.
A program may use at most 128 MiB of HBM per device.

```python
import math
import jax
import jax.numpy as jnp
import numpy as np
from jax import lax

D = 4096
MODES = 64
DOCS = 4
TOK_DEV = 128
SEQLEN = 2048
ROWS = 4
MOST = 64
N_SEQ = 16
N_DP = 4


def draw_decay_rate(key, part):
    uniform_draw = jax.random.uniform(key, (MODES, D), jnp.float32)
    low_log = math.log(0.01)
    high_log = math.log(SEQLEN / 20.0)
    return jnp.exp(low_log + uniform_draw * (high_log - low_log)).astype(jnp.float32)


def block_levels(rng, extent, split, smallest, high):
    factor_of = 1.0
    for dim, blocks in split:
        steps = jax.random.uniform(jax.random.fold_in(jax.random.fold_in(rng, 6), dim), (blocks,), jnp.float32, smallest / len(split), high / len(split))
        factor_of = factor_of * jnp.repeat(jnp.exp(steps), extent[dim] // blocks).reshape((-1,) + (1,) * (len(extent) - 1 - dim))
    return factor_of


def length_profile(count, total, bound, skew):
    portions = [(1 << 20) // math.isqrt(grade ** skew) + 1 for grade in range(2, count + 1)]
    rest, given = total - bound - (count - 1), [1] * (count - 1)
    while rest > 0:
        candidates = [i for i in range(count - 1) if given[i] < bound]
        pool, remaining = sum([portions[i] for i in candidates]), rest
        for i in candidates:
            addition = min(bound - given[i], max(1, remaining * portions[i] // pool), rest)
            given[i] = given[i] + addition
            rest = rest - addition
    return np.array([bound] + given)


def ragged_sizes(rng, count, total, most, slope):
    if count == 2:
        one = jax.random.randint(rng, (), max(1, total - most), min(most, total - 1) + 1)
        return jnp.stack([one, total - one])
    sizes = jnp.asarray(length_profile(count, total, most, slope), jnp.int32)
    twos = (count - 1) // 2
    donor, taker = sizes[1:1 + 2 * twos:2], sizes[2:2 + 2 * twos:2]
    slack = jnp.minimum(donor - 1, most - taker)
    shifted = jax.random.randint(jax.random.fold_in(rng, 1), (twos,), 0, 1 << 20) % (slack + 1)
    sizes = sizes.at[1:1 + 2 * twos:2].set(donor - shifted).at[2:2 + 2 * twos:2].set(taker + shifted)
    return sizes[jax.random.permutation(jax.random.fold_in(rng, 2), count)]


def centred(rng, shape, width, reach, split=(), kind=jnp.bfloat16):
    gain = block_levels(rng, shape, split, -0.22, 0.18) if split else 1.0
    drawn = jax.random.normal(rng, shape, jnp.float32) * width * gain
    return jnp.minimum(jnp.maximum(drawn, -reach), reach).astype(kind)


def setup_inputs(seed: int = 0) -> dict:
    key_of = jax.random.split(jax.random.key(seed), 10)
    return {
        "grad_out": centred(key_of[0], (ROWS, SEQLEN, D), 1.0, 6.0, ((0, 4), (1, 16), (2, 4))),
        "inputs": centred(key_of[1], (ROWS, SEQLEN, D), 1.0, 6.0, ((0, 4), (1, 16), (2, 4))),
        "decay_rate": draw_decay_rate(jax.random.fold_in(key_of[9], 71), 0),
        "frequency": jnp.clip(jax.random.uniform(key_of[3], (MODES, D), jnp.float32, -3.140625, 3.140625), -3.140625, 3.140625),
        "in_proj": centred(key_of[4], (2, MODES, D), 1.0, 6.0, ((2, 4),), jnp.float32),
        "out_proj": centred(key_of[5], (2, MODES, D), (MODES * SEQLEN) ** -0.5, 0.015625, ((2, 4),), jnp.float32),
        "skip_gain": jnp.clip(1.0 + 0.18 * jax.random.normal(key_of[6], (D,), jnp.float32), 0.1, 1.9),
        "doc_lengths": jax.vmap(lambda own: ragged_sizes(own, DOCS, SEQLEN, SEQLEN // 2, 2))(jax.random.split(key_of[7], ROWS)).reshape((ROWS, DOCS)).astype(jnp.int32),
        "piece_lengths": jax.vmap(lambda own: ragged_sizes(own, N_DP, TOK_DEV, MOST, 2))(jax.random.split(key_of[8], ROWS * N_SEQ)).reshape((ROWS, N_SEQ, N_DP)).astype(jnp.int32),
    }


def reference(grad_out, inputs, decay_rate, frequency, in_proj, out_proj, skip_gain, doc_lengths, piece_lengths):
    step_rate = decay_rate / SEQLEN
    pole_re = jnp.exp(-step_rate) * jnp.cos(frequency)
    pole_im = jnp.exp(-step_rate) * jnp.sin(frequency)
    boundary = jnp.cumsum(doc_lengths, axis=1).astype(jnp.int32)[:, :-1]
    position = jnp.arange(SEQLEN, dtype=jnp.int32)
    is_start = jnp.any(position[None, :, None] == boundary[:, None, :], axis=2)
    keep_mask = jnp.where(is_start, 0.0, 1.0).astype(jnp.float32)
    sequence = (jnp.transpose(grad_out.astype(jnp.float32), (1, 0, 2)), jnp.transpose(inputs.astype(jnp.float32), (1, 0, 2)), jnp.transpose(keep_mask, (1, 0)))

    def scan_step(carried, current):
        back_re, back_im, accum_re, accum_im = carried
        grad_now, input_now, keep_now = current
        adjoint_re = out_proj[0][None] * grad_now[:, None, :] + back_re
        adjoint_im = out_proj[1][None] * grad_now[:, None, :] + back_im
        input_grad = lax.optimization_barrier(jnp.sum(in_proj[0][None] * adjoint_re + in_proj[1][None] * adjoint_im, axis=1)) + skip_gain[None] * grad_now
        accum_re = accum_re + lax.optimization_barrier(jnp.sum(input_now[:, None, :] * adjoint_re, axis=0))
        accum_im = accum_im + lax.optimization_barrier(jnp.sum(input_now[:, None, :] * adjoint_im, axis=0))
        keep_factor = keep_now[:, None, None]
        next_re = keep_factor * (pole_re[None] * adjoint_re + pole_im[None] * adjoint_im)
        next_im = keep_factor * (pole_re[None] * adjoint_im - pole_im[None] * adjoint_re)
        return ((next_re, next_im, accum_re, accum_im), input_grad)
    state_zero = jnp.zeros((ROWS, MODES, D), jnp.float32)
    accum_zero = jnp.zeros((MODES, D), jnp.float32)
    final_state, grads = lax.scan(scan_step, (state_zero, state_zero, accum_zero, accum_zero), sequence, reverse=True)
    input_grad = jnp.transpose(grads, (1, 0, 2)).astype(jnp.bfloat16)
    grad_scale = math.sqrt(MODES / (ROWS * SEQLEN))
    grad_b = jnp.stack([final_state[2], final_state[3]]) * grad_scale
    blocks = input_grad.reshape(ROWS, N_SEQ, TOK_DEV, D)
    offsets = (jnp.cumsum(piece_lengths, axis=2) - piece_lengths).astype(jnp.int32)
    slot_ids = jnp.arange(MOST, dtype=jnp.int32)
    row_index = jnp.minimum(offsets[..., None] + slot_ids, TOK_DEV - 1).astype(jnp.int32)
    in_piece = slot_ids < piece_lengths[..., None]
    row_axis = jnp.arange(ROWS, dtype=jnp.int32)[:, None, None, None]
    shard_axis = jnp.arange(N_SEQ, dtype=jnp.int32)[None, :, None, None]
    taken = blocks[row_axis, shard_axis, row_index]
    taken = jnp.where(in_piece[..., None], taken, jnp.zeros((), jnp.bfloat16))
    returned = jnp.transpose(taken, (1, 2, 0, 3, 4))
    return (returned, grad_b)
```

```python
import math

import jax
import jax.numpy as jnp
from jax import lax
from jax.experimental import pallas as pl
from jax.experimental.pallas import tpu as pltpu
from jax.sharding import PartitionSpec as P

MESH = pl.DeviceIdType.MESH
F32 = jnp.float32
BF16 = jnp.bfloat16
I32 = jnp.int32

SEQ = 16
DP = 4
SETS = 2
LEN = 128
WIDE = 512
LANES = 128
GROUP = 32
QUARTER = 32
MODES = 64
ROWS = 16
UNROLL = 16
LAG = 2


def lane_block():
    return lax.broadcasted_iota(I32, (1, LANES), 1) // GROUP


def turn(tile, blocks):
    shift = (blocks % 4) * GROUP
    return tile if shift == 0 else pltpu.roll(tile, shift, 1)


def swap_blocks(tiles):
    block = lane_block()
    out = []
    for g in range(4):
        acc = turn(tiles[0], -g)
        for b in range(1, 4):
            acc = jnp.where(block == b, turn(tiles[b], b - g), acc)
        out.append(acc)
    return out


def spread_blocks(tile):
    block = lane_block()
    turned = [turn(tile, k) for k in range(4)]
    out = []
    for b in range(4):
        acc = turned[(0 - b) % 4]
        for lane in range(1, 4):
            acc = jnp.where(block == lane, turned[(lane - b) % 4], acc)
        out.append(acc)
    return out


def kernel(
    grad_hbm,
    input_hbm,
    decay_hbm,
    freq_hbm,
    in_hbm,
    out_hbm,
    skip_hbm,
    docs,
    pieces,
    ret_ref,
    gb_ref,
    grad_v,
    input_v,
    param_v,
    skip_v,
    send_a,
    recv_a,
    coef,
    proj,
    skips,
    state,
    total,
    gd,
    ud,
    partial,
    send_d,
    recv_d,
    rows_d,
    pick,
    send_y,
    g_dp,
    g_seq,
    load_sem,
    a_send,
    a_recv,
    d_send,
    d_recv,
    y_send,
    y_recv,
    p_send,
    p_recv,
    s_send,
    s_recv,
    c_send,
    c_recv,
):
    me = lax.axis_index("seq")
    row = lax.axis_index("dp")
    core = lax.rem(me, 2)
    chip = me // 2
    block = lane_block()
    own_block = lax.rem(me, 4)

    loads = []

    def load(src, dst):
        copy = pltpu.make_async_copy(src, dst, load_sem.at[len(loads)])
        copy.start()
        loads.append(copy)

    for c in range(SETS):
        wide = pl.ds(c * WIDE, WIDE)
        load(grad_hbm.at[0, :, wide], grad_v.at[c])
        load(input_hbm.at[0, :, wide], input_v.at[c])
    for c in range(SETS):
        tile = pl.ds(pl.multiple_of((4 * c + me // 4) * LANES, LANES), LANES)
        load(decay_hbm.at[:, tile], param_v.at[c, 0])
        load(freq_hbm.at[:, tile], param_v.at[c, 1])
        load(in_hbm.at[:, :, tile], param_v.at[c, pl.ds(2, 2)])
        load(out_hbm.at[:, :, tile], param_v.at[c, pl.ds(4, 2)])
        load(skip_hbm.at[:, tile], skip_v.at[c])

    barrier = pltpu.get_barrier_semaphore()

    def greet(k, _):
        pl.semaphore_signal(
            barrier, inc=1, device_id={"seq": lax.rem(me + k, SEQ)}, device_id_type=MESH
        )
        return 0

    lax.fori_loop(1, SEQ, greet, 0)
    for k in range(1, DP):
        pl.semaphore_signal(
            barrier, inc=1, device_id={"dp": lax.rem(row + k, DP)}, device_id_type=MESH
        )

    def copy_a(c, there, slot):
        return pltpu.make_async_remote_copy(
            src_ref=send_a.at[c, there],
            dst_ref=recv_a.at[c, slot],
            send_sem=a_send.at[c, there],
            recv_sem=a_recv.at[c, slot],
            device_id={"seq": there},
            device_id_type=MESH,
        )

    def pack(c):
        loads[2 * c].wait()
        loads[2 * c + 1].wait()
        for t in range(4):
            cols = slice(t * LANES, (t + 1) * LANES)
            for k, source in enumerate((grad_v, input_v)):
                tiles = [
                    source[c, q * QUARTER : (q + 1) * QUARTER, cols].astype(F32) for q in range(4)
                ]
                for g, tile in enumerate(swap_blocks(tiles)):
                    send_a[c, 4 * t + g, k * QUARTER : (k + 1) * QUARTER, :] = tile.astype(BF16)

    def launch(c):
        def one(k, _):
            copy_a(c, lax.rem(me + k, SEQ), me).start()
            return 0

        lax.fori_loop(1, SEQ, one, 0)
        recv_a[c, me] = send_a[c, me]

    pack(0)
    pl.semaphore_wait(barrier, SEQ - 1 + DP - 1)
    launch(0)
    pack(1)
    launch(1)

    for copy in loads[2 * SETS :]:
        copy.wait()

    def own(tile, rows):
        acc = pltpu.roll(tile[:rows], lax.rem(4 - own_block, 4) * GROUP, 1)
        for q in range(1, 4):
            part = tile[:rows] if rows == 1 else tile[q * rows : (q + 1) * rows]
            turned = pltpu.roll(part, lax.rem(4 + q - own_block, 4) * GROUP, 1)
            acc = jnp.where(block == q, turned, acc)
        return acc

    for c in range(SETS):
        decay, freq, b_re, b_im, c_re, c_im = [own(param_v[c, k], ROWS) for k in range(6)]
        size = jnp.exp(-(decay / (SEQ * LEN)))
        coef[c, 0, 0] = size * jnp.cos(freq)
        coef[c, 0, 1] = -(size * jnp.sin(freq))
        coef[c, 1] = jnp.zeros((2, ROWS, LANES), F32)
        proj[c, 0] = b_re * c_re + b_im * c_im
        proj[c, 1] = b_im * c_re - b_re * c_im
        proj[c, 2] = c_re
        proj[c, 3] = c_im
        skips[c] = own(skip_v[c], 1)

    first = I32(0)
    slot = lax.broadcasted_iota(I32, (64, LEN), 0)
    place = lax.broadcasted_iota(I32, (64, LEN), 1)
    for j in range(DP):
        length = pieces[0, 0, j]
        chosen = (place - slot == first) & (slot < length)
        pick[j * 64 : (j + 1) * 64, :] = jnp.where(chosen, 1.0, 0.0).astype(BF16)
        first = first + length

    starts = [docs[0, 0]]
    for k in range(1, 3):
        starts.append(starts[-1] + docs[0, k])

    def copy_d(c, there, slot):
        return pltpu.make_async_remote_copy(
            src_ref=send_d.at[c, there],
            dst_ref=recv_d.at[c, slot],
            send_sem=d_send.at[c, there],
            recv_sem=d_recv.at[c, slot],
            device_id={"seq": there},
            device_id_type=MESH,
        )

    def scan_segment(c, t):
        @pl.when(t != me)
        def _():
            copy_a(c, t, t).wait_recv()

        for k, dest in enumerate((gd, ud)):
            tile = recv_a[c, t, k * QUARTER : (k + 1) * QUARTER, :].astype(F32)
            for q, spread in enumerate(spread_blocks(tile)):
                dest[q * QUARTER : (q + 1) * QUARTER, :] = spread

        def positions(b, carry):
            x, y, sx, sy = carry
            base = pl.multiple_of(LEN - (b + 1) * UNROLL, UNROLL)
            whole = t * LEN + base
            for i in range(UNROLL - 1, -1, -1):
                after = whole + (i + 1)
                cut = (after == starts[0]) | (after == starts[1]) | (after == starts[2])
                cut = cut.astype(I32)
                a_re = coef[c, cut, 0]
                a_im = coef[c, cut, 1]
                g = gd[pl.ds(base + i, 1), :]
                u = ud[pl.ds(base + i, 1), :]
                x, y = a_re * x + (g - a_im * y), a_re * y + a_im * x
                sx = sx + u * x
                sy = sy + u * y
                d = proj[c, 0] * x + proj[c, 1] * y
                partial[pl.ds(pl.multiple_of((base + i) * 8, 8), 8), :] = d[:8] + d[8:]
            return x, y, sx, sy

        carry = (state[0], state[1], total[0], total[1])
        carry = lax.fori_loop(0, LEN // UNROLL, positions, carry)
        state[0], state[1], total[0], total[1] = carry

        message = jnp.zeros((QUARTER, LANES), F32)
        for q in range(4):
            tiles = []
            for p in range(QUARTER // 8):
                at = (q * QUARTER + p * 8) * 8
                terms = [partial[pl.ds(at + k, 8, stride=8), :] for k in range(8)]
                while len(terms) > 1:
                    terms = [terms[k] + terms[k + 1] for k in range(0, len(terms), 2)]
                tiles.append(terms[0])
            part = jnp.concatenate(tiles, axis=0)
            part = part + turn(part, 2)
            part = part + turn(part, 1)
            part = part + skips[c] * gd[q * QUARTER : (q + 1) * QUARTER, :]
            message = jnp.where(block == q, part, message)
        message = message.astype(BF16)

        @pl.when(t != me)
        def _():
            send_d[c, t] = message
            copy_d(c, t, me).start()

        @pl.when(t == me)
        def _():
            recv_d[c, me] = message

    def copy_y(c, there, slot):
        cols = pl.ds(pl.multiple_of(c * WIDE, WIDE), WIDE)
        return pltpu.make_async_remote_copy(
            src_ref=send_y.at[c, there],
            dst_ref=ret_ref.at[slot, :, cols],
            send_sem=y_send.at[c, there],
            recv_sem=y_recv.at[c, slot],
            device_id={"dp": there},
            device_id_type=MESH,
        )

    def deliver(c):
        def arrived(k, _):
            other = lax.rem(me + k, SEQ)
            copy_d(c, other, other).wait_recv()
            return 0

        lax.fori_loop(1, SEQ, arrived, 0)
        for t in range(4):
            tiles = [recv_d[c, 4 * t + g].astype(F32) for g in range(4)]
            for q, tile in enumerate(swap_blocks(tiles)):
                rows_d[q * QUARTER : (q + 1) * QUARTER, t * LANES : (t + 1) * LANES] = tile.astype(
                    BF16
                )
        for j in range(DP):
            sent = jnp.dot(
                pick[j * 64 : (j + 1) * 64, :], rows_d[...], preferred_element_type=F32
            ).astype(BF16)
            send_y[c, j] = sent
        for k in range(1, DP):
            copy_y(c, lax.rem(row + k, DP), row).start()
        cols = pl.ds(pl.multiple_of(c * WIDE, WIDE), WIDE)
        ret_ref[row, :, cols] = send_y[c, row]

    def copy_p(c, there, slot):
        return pltpu.make_async_remote_copy(
            src_ref=g_dp.at[c, row],
            dst_ref=g_dp.at[c, slot],
            send_sem=p_send.at[c, there],
            recv_sem=p_recv.at[c, slot],
            device_id={"dp": there},
            device_id_type=MESH,
        )

    def copy_s(c, there, slot):
        return pltpu.make_async_remote_copy(
            src_ref=g_seq.at[c, core, chip],
            dst_ref=g_seq.at[c, core, slot],
            send_sem=s_send.at[c, there],
            recv_sem=s_recv.at[c, slot],
            device_id={"seq": there * 2 + core},
            device_id_type=MESH,
        )

    def copy_c(c, half):
        return pltpu.make_async_remote_copy(
            src_ref=g_seq.at[c, half],
            dst_ref=g_seq.at[c, half],
            send_sem=c_send.at[c],
            recv_sem=c_recv.at[c],
            device_id={"seq": chip * 2 + (1 - core)},
            device_id_type=MESH,
        )

    def sum_own(c):
        sx, sy = total[0], total[1]
        c_re, c_im = proj[c, 2], proj[c, 3]
        g_dp[c, row, 0] = c_re * sx - c_im * sy
        g_dp[c, row, 1] = c_re * sy + c_im * sx
        for k in range(1, DP):
            copy_p(c, lax.rem(row + k, DP), row).start()

    def sum_rows(c):
        for k in range(1, DP):
            other = lax.rem(row + k, DP)
            copy_p(c, other, other).wait_recv()
        scale = math.sqrt(MODES / (DP * SEQ * LEN))
        g_seq[c, core, chip] = ((g_dp[c, 0] + g_dp[c, 1]) + (g_dp[c, 2] + g_dp[c, 3])) * scale
        for k in range(1, SEQ // 2):
            copy_s(c, lax.rem(chip + k, SEQ // 2), chip).start()

    def to_sibling(c):
        for k in range(1, SEQ // 2):
            other = lax.rem(chip + k, SEQ // 2)
            copy_s(c, other, other).wait_recv()
        copy_c(c, core).start()

    def write_sums(c):
        copy_c(c, 1 - core).wait_recv()
        for t in range(4):
            for k in range(2):
                tiles = [g_seq[c, g % 2, (4 * t + g) // 2, k] for g in range(4)]
                for q, tile in enumerate(swap_blocks(tiles)):
                    at = c * WIDE + t * LANES
                    gb_ref[k, q * ROWS : (q + 1) * ROWS, at : at + LANES] = tile

    def step(n, _):
        c = n // SEQ
        t = SEQ - 1 - lax.rem(n, SEQ)

        @pl.when(n == SEQ)
        def _():
            sum_own(0)

        @pl.when(n == SEQ + 4)
        def _():
            sum_rows(0)

        @pl.when(n == SEQ + 9)
        def _():
            to_sibling(0)

        @pl.when(n == SEQ + 12)
        def _():
            write_sums(0)

        @pl.when(t == SEQ - 1)
        def _():
            state[...] = jnp.zeros_like(state)
            total[...] = jnp.zeros_like(total)

        scan_segment(c, t)
        late = n - LAG - (SEQ - 1 - me)

        @pl.when((late == 0) | (late == SEQ))
        def _():
            deliver(late // SEQ)

        return 0

    lax.fori_loop(0, SETS * SEQ, step, 0)
    sum_own(1)

    @pl.when(me < LAG)
    def _():
        deliver(1)

    sum_rows(1)
    to_sibling(1)
    write_sums(1)

    for c in range(SETS):
        for k in range(1, DP):
            other = lax.rem(row + k, DP)
            copy_y(c, other, other).wait_recv()
            copy_y(c, other, row).wait_send()
            copy_p(c, other, row).wait_send()
        for k in range(1, SEQ // 2):
            copy_s(c, lax.rem(chip + k, SEQ // 2), chip).wait_send()
        copy_c(c, core).wait_send()

        def left(k, _):
            other = lax.rem(me + k, SEQ)
            copy_a(c, other, me).wait_send()
            copy_d(c, other, me).wait_send()
            return 0

        lax.fori_loop(1, SEQ, left, 0)


def shards(
    grad_out,
    inputs,
    decay_rate,
    frequency,
    in_proj,
    out_proj,
    skip_gain,
    doc_lengths,
    piece_lengths,
):
    anywhere = pl.BlockSpec(memory_space=pl.ANY)
    scalars = pl.BlockSpec(memory_space=pltpu.SMEM)
    vmem = pl.BlockSpec(memory_space=pltpu.VMEM)
    dma = pltpu.SemaphoreType.DMA
    returned, grad_b = pl.pallas_call(
        kernel,
        out_shape=(
            jax.ShapeDtypeStruct((DP, 64, SETS * WIDE), BF16),
            jax.ShapeDtypeStruct((2, MODES, SETS * WIDE), F32),
        ),
        in_specs=[anywhere] * 7 + [scalars] * 2,
        out_specs=(vmem, vmem),
        scratch_shapes=[
            pltpu.VMEM((SETS, LEN, WIDE), BF16),
            pltpu.VMEM((SETS, LEN, WIDE), BF16),
            pltpu.VMEM((SETS, 6, MODES, LANES), F32),
            pltpu.VMEM((SETS, 1, LANES), F32),
            pltpu.VMEM((SETS, SEQ, 2 * QUARTER, LANES), BF16),
            pltpu.VMEM((SETS, SEQ, 2 * QUARTER, LANES), BF16),
            pltpu.VMEM((SETS, 2, 2, ROWS, LANES), F32),
            pltpu.VMEM((SETS, 4, ROWS, LANES), F32),
            pltpu.VMEM((SETS, 1, LANES), F32),
            pltpu.VMEM((2, ROWS, LANES), F32),
            pltpu.VMEM((2, ROWS, LANES), F32),
            pltpu.VMEM((LEN, LANES), F32),
            pltpu.VMEM((LEN, LANES), F32),
            pltpu.VMEM((LEN * 8, LANES), F32),
            pltpu.VMEM((SETS, SEQ, QUARTER, LANES), BF16),
            pltpu.VMEM((SETS, SEQ, QUARTER, LANES), BF16),
            pltpu.VMEM((LEN, WIDE), BF16),
            pltpu.VMEM((DP * 64, LEN), BF16),
            pltpu.VMEM((SETS, DP, 64, WIDE), BF16),
            pltpu.VMEM((SETS, DP, 2, ROWS, LANES), F32),
            pltpu.VMEM((SETS, 2, SEQ // 2, 2, ROWS, LANES), F32),
            dma((7 * SETS,)),
            dma((SETS, SEQ)),
            dma((SETS, SEQ)),
            dma((SETS, SEQ)),
            dma((SETS, SEQ)),
            dma((SETS, DP)),
            dma((SETS, DP)),
            dma((SETS, DP)),
            dma((SETS, DP)),
            dma((SETS, SEQ // 2)),
            dma((SETS, SEQ // 2)),
            dma((SETS,)),
            dma((SETS,)),
        ],
        compiler_params=pltpu.CompilerParams(
            collective_id=0, has_side_effects=True, vmem_limit_bytes=32 << 20
        ),
        cost_estimate=pl.CostEstimate(
            flops=15 * 128 * 64 * 1024, bytes_accessed=4 << 20, transcendentals=0
        ),
        name="scan_rows",
    )(
        grad_out,
        inputs,
        decay_rate,
        frequency,
        in_proj,
        out_proj,
        skip_gain[None],
        doc_lengths,
        piece_lengths,
    )
    return returned[None, None], grad_b


def solution(mesh):
    return jax.shard_map(
        shards,
        mesh=mesh,
        in_specs=(
            P("dp", "seq", "ch"),
            P("dp", "seq", "ch"),
            P(None, "ch"),
            P(None, "ch"),
            P(None, None, "ch"),
            P(None, None, "ch"),
            P("ch"),
            P("dp", None),
            P("dp", "seq", None),
        ),
        out_specs=(P("seq", "dp", None, None, "ch"), P(None, None, "ch")),
        check_vma=False,
    )
```

```python
import math

import jax
import jax.numpy as jnp
from jax import lax
from jax.experimental import pallas as pl
from jax.experimental.pallas import tpu as pltpu
from jax.sharding import PartitionSpec as P

MESH = pl.DeviceIdType.MESH
F32 = jnp.float32
BF16 = jnp.bfloat16
I32 = jnp.int32

SEQ = 16
DP = 4
SETS = 2
LEN = 128
WIDE = 512
LANES = 128
GROUP = 32
QUARTER = 32
MODES = 64
ROWS = 16
HALF = SEQ // 2


def lane_block():
    return lax.broadcasted_iota(I32, (1, LANES), 1) // GROUP


def turn(tile, blocks):
    shift = (blocks % 4) * GROUP
    return tile if shift == 0 else pltpu.roll(tile, shift, 1)


def interleave(tile):
    return [
        jnp.concatenate([tile[32 * r + 8 * b : 32 * r + 8 * b + 8] for r in range(4)], axis=0)
        for b in range(4)
    ]


def fold_rows(tiles):
    place = lax.broadcasted_iota(I32, (8, 1), 0)
    for step in (1, 2, 4):
        first = (place & step) == 0
        out = []
        half = len(tiles) // 2
        pairs = [(2 * k, 2 * k + 1) for k in range(half)]
        for one, two in pairs:
            kept = jnp.where(first, tiles[one], tiles[two])
            moved = jnp.where(first, tiles[two], tiles[one])
            out.append(kept + pltpu.roll(moved, 8 - step, 0))
        tiles = out
    return tiles[0]


def fold_blocks(tiles):
    block = lane_block()
    for step in (1, 2):
        first = (block & step) == 0
        out = []
        for one, two in [(2 * k, 2 * k + 1) for k in range(len(tiles) // 2)]:
            kept = jnp.where(first, tiles[one], tiles[two])
            moved = jnp.where(first, tiles[two], tiles[one])
            out.append(kept + turn(moved, -step))
        tiles = out
    return tiles[0]


def swap_blocks(tiles):
    block = lane_block()
    out = []
    for g in range(4):
        acc = turn(tiles[0], -g)
        for b in range(1, 4):
            acc = jnp.where(block == b, turn(tiles[b], b - g), acc)
        out.append(acc)
    return out


def spread_blocks(tile):
    block = lane_block()
    turned = [turn(tile, k) for k in range(4)]
    out = []
    for b in range(4):
        acc = turned[(0 - b) % 4]
        for lane in range(1, 4):
            acc = jnp.where(block == lane, turned[(lane - b) % 4], acc)
        out.append(acc)
    return out


def kernel(
    grad_hbm,
    input_hbm,
    decay_hbm,
    freq_hbm,
    in_hbm,
    out_hbm,
    skip_hbm,
    docs,
    pieces,
    ret_ref,
    gb_ref,
    grad_v,
    input_v,
    param_v,
    skip_v,
    send_a,
    recv_a,
    coef,
    proj,
    skips,
    state,
    total,
    gd,
    ud,
    partial,
    send_d,
    recv_d,
    rows_d,
    pick,
    send_y,
    g_dp,
    g_all,
    load_sem,
    a_send,
    a_recv,
    d_send,
    d_recv,
    y_send,
    y_recv,
    p_send,
    p_recv,
    s_send,
    s_recv,
):
    me = lax.axis_index("seq")
    row = lax.axis_index("dp")
    block = lane_block()
    own_block = lax.rem(me, 4)

    loads = []

    def load(src, dst):
        copy = pltpu.make_async_copy(src, dst, load_sem.at[len(loads)])
        copy.start()
        loads.append(copy)

    for c in range(SETS):
        wide = pl.ds(c * WIDE, WIDE)
        load(grad_hbm.at[0, :, wide], grad_v.at[c])
        load(input_hbm.at[0, :, wide], input_v.at[c])
    for c in range(SETS):
        tile = pl.ds(pl.multiple_of((4 * c + me // 4) * LANES, LANES), LANES)
        load(decay_hbm.at[:, tile], param_v.at[c, 0])
        load(freq_hbm.at[:, tile], param_v.at[c, 1])
        load(in_hbm.at[:, :, tile], param_v.at[c, pl.ds(2, 2)])
        load(out_hbm.at[:, :, tile], param_v.at[c, pl.ds(4, 2)])
        load(skip_hbm.at[:, tile], skip_v.at[c])

    barrier = pltpu.get_barrier_semaphore()

    def greet(k, _):
        pl.semaphore_signal(
            barrier, inc=1, device_id={"seq": lax.rem(me + k, SEQ)}, device_id_type=MESH
        )
        return 0

    lax.fori_loop(1, SEQ, greet, 0)
    for k in range(1, DP):
        pl.semaphore_signal(
            barrier, inc=1, device_id={"dp": lax.rem(row + k, DP)}, device_id_type=MESH
        )

    def copy_a(c, there, slot):
        return pltpu.make_async_remote_copy(
            src_ref=send_a.at[c, there],
            dst_ref=recv_a.at[c, slot],
            send_sem=a_send.at[c, there],
            recv_sem=a_recv.at[c, slot],
            device_id={"seq": there},
            device_id_type=MESH,
        )

    def pack(c):
        loads[2 * c].wait()
        loads[2 * c + 1].wait()
        for t in range(4):
            cols = slice(t * LANES, (t + 1) * LANES)
            for k, source in enumerate((grad_v, input_v)):
                tiles = interleave(source[c, :, cols].astype(F32))
                for g, tile in enumerate(swap_blocks(tiles)):
                    send_a[c, 4 * t + g, k * QUARTER : (k + 1) * QUARTER, :] = tile.astype(BF16)

    def launch(c):
        def one(k, _):
            copy_a(c, lax.rem(me + k, SEQ), me).start()
            return 0

        lax.fori_loop(1, SEQ, one, 0)
        recv_a[c, me] = send_a[c, me]

    pack(0)
    pl.semaphore_wait(barrier, SEQ - 1 + DP - 1)
    launch(0)
    pack(1)
    launch(1)

    for copy in loads[2 * SETS :]:
        copy.wait()

    def own(tile, rows):
        acc = pltpu.roll(tile[:rows], lax.rem(4 - own_block, 4) * GROUP, 1)
        for q in range(1, 4):
            part = tile[:rows] if rows == 1 else tile[q * rows : (q + 1) * rows]
            turned = pltpu.roll(part, lax.rem(4 + q - own_block, 4) * GROUP, 1)
            acc = jnp.where(block == q, turned, acc)
        return acc

    for c in range(SETS):
        decay, freq, b_re, b_im, c_re, c_im = [own(param_v[c, k], ROWS) for k in range(6)]
        size = jnp.exp(-(decay / (SEQ * LEN)))
        coef[c, 0, 0] = size * jnp.cos(freq)
        coef[c, 0, 1] = -(size * jnp.sin(freq))
        coef[c, 1] = jnp.zeros((2, ROWS, LANES), F32)
        proj[c, 0] = b_re * c_re + b_im * c_im
        proj[c, 1] = b_im * c_re - b_re * c_im
        proj[c, 2] = c_re
        proj[c, 3] = c_im
        skips[c] = own(skip_v[c], 1)

    first = I32(0)
    slot = lax.broadcasted_iota(I32, (64, LEN), 0)
    place = lax.broadcasted_iota(I32, (64, LEN), 1)
    for j in range(DP):
        length = pieces[0, 0, j]
        chosen = (place - slot == first) & (slot < length)
        pick[j * 64 : (j + 1) * 64, :] = jnp.where(chosen, 1.0, 0.0).astype(BF16)
        first = first + length

    starts = [docs[0, 0]]
    for k in range(1, 3):
        starts.append(starts[-1] + docs[0, k])

    def copy_d(c, there, slot):
        return pltpu.make_async_remote_copy(
            src_ref=send_d.at[c, there],
            dst_ref=recv_d.at[c, slot],
            send_sem=d_send.at[c, there],
            recv_sem=d_recv.at[c, slot],
            device_id={"seq": there},
            device_id_type=MESH,
        )

    def send_home(c, t):
        @pl.when(t != me)
        def _():
            copy_d(c, t, me).start()

    def scan_segment(c, t):
        @pl.when(t != me)
        def _():
            copy_a(c, t, t).wait_recv()

        for k, dest in enumerate((gd, ud)):
            tile = recv_a[c, t, k * QUARTER : (k + 1) * QUARTER, :].astype(F32)
            for b, spread in enumerate(spread_blocks(tile)):
                for r in range(4):
                    at = 32 * r + 8 * b
                    dest[at : at + 8, :] = spread[8 * r : 8 * r + 8]

        x, y, sx, sy = state[0], state[1], total[0], total[1]
        sums = []
        for i in range(LEN - 1, -1, -1):
            after = t * LEN + (i + 1)
            cut = (after == starts[0]) | (after == starts[1]) | (after == starts[2])
            cut = cut.astype(I32)
            a_re = coef[c, cut, 0]
            a_im = coef[c, cut, 1]
            g = gd[i : i + 1, :]
            u = ud[i : i + 1, :]
            x, y = a_re * x + (g - a_im * y), a_re * y + a_im * x
            sx = sx + u * x
            sy = sy + u * y
            d = proj[c, 0] * x + proj[c, 1] * y
            sums.insert(0, d[:8] + d[8:])
            if i % 8 == 0:
                partial[i : i + 8, :] = fold_rows(sums)
                sums = []
        state[0], state[1], total[0], total[1] = x, y, sx, sy

        message = fold_blocks(interleave(partial[...]))
        message = message + skips[c] * recv_a[c, t, :QUARTER, :].astype(F32)
        message = message.astype(BF16)

        @pl.when(t != me)
        def _():
            send_d[c, t] = message

        @pl.when(t == me)
        def _():
            recv_d[c, me] = message

    def copy_y(c, there, slot):
        cols = pl.ds(pl.multiple_of(c * WIDE, WIDE), WIDE)
        return pltpu.make_async_remote_copy(
            src_ref=send_y.at[c, there],
            dst_ref=ret_ref.at[slot, :, cols],
            send_sem=y_send.at[c, there],
            recv_sem=y_recv.at[c, slot],
            device_id={"dp": there},
            device_id_type=MESH,
        )

    def deliver(c):
        def arrived(k, _):
            other = lax.rem(me + k, SEQ)
            copy_d(c, other, other).wait_recv()
            return 0

        lax.fori_loop(1, SEQ, arrived, 0)
        for t in range(4):
            tiles = [recv_d[c, 4 * t + g].astype(F32) for g in range(4)]
            tiles = swap_blocks(tiles)
            whole = [tiles[b][8 * r : 8 * r + 8] for r in range(4) for b in range(4)]
            whole = jnp.concatenate(whole, axis=0)
            rows_d[:, t * LANES : (t + 1) * LANES] = whole.astype(BF16)
        for j in range(DP):
            sent = jnp.dot(
                pick[j * 64 : (j + 1) * 64, :], rows_d[...], preferred_element_type=F32
            ).astype(BF16)
            send_y[c, j] = sent
        for k in range(1, DP):
            copy_y(c, lax.rem(row + k, DP), row).start()
        cols = pl.ds(pl.multiple_of(c * WIDE, WIDE), WIDE)
        ret_ref[row, :, cols] = send_y[c, row]

    def copy_p(c, there, slot):
        return pltpu.make_async_remote_copy(
            src_ref=g_dp.at[c, row],
            dst_ref=g_dp.at[c, slot],
            send_sem=p_send.at[c, there],
            recv_sem=p_recv.at[c, slot],
            device_id={"dp": there},
            device_id_type=MESH,
        )

    def copy_s(c, there, slot):
        return pltpu.make_async_remote_copy(
            src_ref=g_all.at[c, me],
            dst_ref=g_all.at[c, slot],
            send_sem=s_send.at[c, there],
            recv_sem=s_recv.at[c, slot],
            device_id={"seq": there},
            device_id_type=MESH,
        )

    def sum_own(c):
        sx, sy = total[0], total[1]
        c_re, c_im = proj[c, 2], proj[c, 3]
        g_dp[c, row, 0] = c_re * sx - c_im * sy
        g_dp[c, row, 1] = c_re * sy + c_im * sx
        for k in range(1, DP):
            copy_p(c, lax.rem(row + k, DP), row).start()

    def sum_rows(c):
        for k in range(1, DP):
            other = lax.rem(row + k, DP)
            copy_p(c, other, other).wait_recv()
        scale = math.sqrt(MODES / (DP * SEQ * LEN))
        g_all[c, me] = ((g_dp[c, 0] + g_dp[c, 1]) + (g_dp[c, 2] + g_dp[c, 3])) * scale

        def one(k, _):
            copy_s(c, lax.rem(me + k, SEQ), me).start()
            return 0

        lax.fori_loop(1, SEQ, one, 0)

    def write_sums(c):
        def one(k, _):
            other = lax.rem(me + k, SEQ)
            copy_s(c, other, other).wait_recv()
            return 0

        lax.fori_loop(1, SEQ, one, 0)
        for t in range(4):
            cols = slice(c * WIDE + t * LANES, c * WIDE + (t + 1) * LANES)
            for k in range(2):
                tiles = [g_all[c, 4 * t + g, k] for g in range(4)]
                for q, tile in enumerate(swap_blocks(tiles)):
                    gb_ref[k, q * ROWS : (q + 1) * ROWS, cols] = tile

    def step(n, _):
        c = n // SEQ
        t = SEQ - 1 - lax.rem(n, SEQ)

        @pl.when(n == SEQ)
        def _():
            sum_own(0)

        @pl.when(n == SEQ + 4)
        def _():
            sum_rows(0)

        last = n - SEQ

        @pl.when((last >= 0) & (last < HALF))
        def _():
            send_home(0, lax.rem(me + 2 * last + 1, SEQ))
            send_home(0, lax.rem(me + 2 * last + 2, SEQ))

        @pl.when(t == SEQ - 1)
        def _():
            state[...] = jnp.zeros_like(state)
            total[...] = jnp.zeros_like(total)

        scan_segment(c, t)

        @pl.when((last >= HALF - 1) & (last < HALF + 3))
        def _():
            for k in range(2):
                send_home(1, HALF + lax.rem(me + 2 * (last + 1) + k, HALF))

        @pl.when((last >= HALF + 3) & (last < HALF + 5))
        def _():
            for k in range(2):
                send_home(1, HALF // 2 + lax.rem(me + 2 * (last + 1) + k, HALF // 2))

        @pl.when(last == HALF + 5)
        def _():
            for k in range(2):
                send_home(1, 2 + lax.rem(me + k, 2))

        @pl.when(last >= HALF + 6)
        def _():
            send_home(1, t)

        @pl.when(last == SEQ - 3)
        def _():
            deliver(0)

        @pl.when((last == SEQ - 2) & (me >= HALF))
        def _():
            deliver(1)

        return 0

    lax.fori_loop(0, SETS * SEQ, step, 0)
    sum_own(1)
    write_sums(0)
    sum_rows(1)

    @pl.when(me < HALF)
    def _():
        deliver(1)

    write_sums(1)

    for c in range(SETS):
        for k in range(1, DP):
            other = lax.rem(row + k, DP)
            copy_y(c, other, other).wait_recv()
            copy_y(c, other, row).wait_send()
            copy_p(c, other, row).wait_send()

        def left(k, _):
            other = lax.rem(me + k, SEQ)
            copy_a(c, other, me).wait_send()
            copy_d(c, other, me).wait_send()
            copy_s(c, other, me).wait_send()
            return 0

        lax.fori_loop(1, SEQ, left, 0)


def shards(
    grad_out,
    inputs,
    decay_rate,
    frequency,
    in_proj,
    out_proj,
    skip_gain,
    doc_lengths,
    piece_lengths,
):
    anywhere = pl.BlockSpec(memory_space=pl.ANY)
    scalars = pl.BlockSpec(memory_space=pltpu.SMEM)
    vmem = pl.BlockSpec(memory_space=pltpu.VMEM)
    dma = pltpu.SemaphoreType.DMA
    returned, grad_b = pl.pallas_call(
        kernel,
        out_shape=(
            jax.ShapeDtypeStruct((DP, 64, SETS * WIDE), BF16),
            jax.ShapeDtypeStruct((2, MODES, SETS * WIDE), F32),
        ),
        in_specs=[anywhere] * 7 + [scalars] * 2,
        out_specs=(vmem, vmem),
        scratch_shapes=[
            pltpu.VMEM((SETS, LEN, WIDE), BF16),
            pltpu.VMEM((SETS, LEN, WIDE), BF16),
            pltpu.VMEM((SETS, 6, MODES, LANES), F32),
            pltpu.VMEM((SETS, 1, LANES), F32),
            pltpu.VMEM((SETS, SEQ, 2 * QUARTER, LANES), BF16),
            pltpu.VMEM((SETS, SEQ, 2 * QUARTER, LANES), BF16),
            pltpu.VMEM((SETS, 2, 2, ROWS, LANES), F32),
            pltpu.VMEM((SETS, 4, ROWS, LANES), F32),
            pltpu.VMEM((SETS, 1, LANES), F32),
            pltpu.VMEM((2, ROWS, LANES), F32),
            pltpu.VMEM((2, ROWS, LANES), F32),
            pltpu.VMEM((LEN, LANES), F32),
            pltpu.VMEM((LEN, LANES), F32),
            pltpu.VMEM((LEN, LANES), F32),
            pltpu.VMEM((SETS, SEQ, QUARTER, LANES), BF16),
            pltpu.VMEM((SETS, SEQ, QUARTER, LANES), BF16),
            pltpu.VMEM((LEN, WIDE), BF16),
            pltpu.VMEM((DP * 64, LEN), BF16),
            pltpu.VMEM((SETS, DP, 64, WIDE), BF16),
            pltpu.VMEM((SETS, DP, 2, ROWS, LANES), F32),
            pltpu.VMEM((SETS, SEQ, 2, ROWS, LANES), F32),
            dma((7 * SETS,)),
            dma((SETS, SEQ)),
            dma((SETS, SEQ)),
            dma((SETS, SEQ)),
            dma((SETS, SEQ)),
            dma((SETS, DP)),
            dma((SETS, DP)),
            dma((SETS, DP)),
            dma((SETS, DP)),
            dma((SETS, SEQ)),
            dma((SETS, SEQ)),
        ],
        compiler_params=pltpu.CompilerParams(
            collective_id=0, has_side_effects=True, vmem_limit_bytes=62 << 20
        ),
        cost_estimate=pl.CostEstimate(
            flops=15 * 128 * 64 * 1024, bytes_accessed=4 << 20, transcendentals=0
        ),
        name="scan_rows",
    )(
        grad_out,
        inputs,
        decay_rate,
        frequency,
        in_proj,
        out_proj,
        skip_gain[None],
        doc_lengths,
        piece_lengths,
    )
    return returned[None, None], grad_b


def solution(mesh):
    return jax.shard_map(
        shards,
        mesh=mesh,
        in_specs=(
            P("dp", "seq", "ch"),
            P("dp", "seq", "ch"),
            P(None, "ch"),
            P(None, "ch"),
            P(None, None, "ch"),
            P(None, None, "ch"),
            P("ch"),
            P("dp", None),
            P("dp", "seq", None),
        ),
        out_specs=(P("seq", "dp", None, None, "ch"), P(None, None, "ch")),
        check_vma=False,
    )
```

```python
import math

import jax
import jax.numpy as jnp
from jax import lax
from jax.experimental import pallas as pl
from jax.experimental.pallas import tpu as pltpu
from jax.sharding import PartitionSpec as P

MESH = pl.DeviceIdType.MESH
F32 = jnp.float32
BF16 = jnp.bfloat16
I32 = jnp.int32

SEQ = 16
DP = 4
SETS = 2
LEN = 128
WIDE = 512
LANES = 128
GROUP = 32
QUARTER = 32
MODES = 64
ROWS = 16
HALF = SEQ // 2
SECOND = 3


def lane_block():
    return lax.broadcasted_iota(I32, (1, LANES), 1) // GROUP


def turn(tile, blocks):
    shift = (blocks % 4) * GROUP
    return tile if shift == 0 else pltpu.roll(tile, shift, 1)


def interleave(tile):
    return [
        jnp.concatenate([tile[32 * r + 8 * b : 32 * r + 8 * b + 8] for r in range(4)], axis=0)
        for b in range(4)
    ]


def fold_rows(tiles):
    place = lax.broadcasted_iota(I32, (8, 1), 0)
    for step in (1, 2, 4):
        first = (place & step) == 0
        out = []
        half = len(tiles) // 2
        pairs = [(2 * k, 2 * k + 1) for k in range(half)]
        for one, two in pairs:
            kept = jnp.where(first, tiles[one], tiles[two])
            moved = jnp.where(first, tiles[two], tiles[one])
            out.append(kept + pltpu.roll(moved, 8 - step, 0))
        tiles = out
    return tiles[0]


def fold_blocks(tiles):
    block = lane_block()
    for step in (1, 2):
        first = (block & step) == 0
        out = []
        for one, two in [(2 * k, 2 * k + 1) for k in range(len(tiles) // 2)]:
            kept = jnp.where(first, tiles[one], tiles[two])
            moved = jnp.where(first, tiles[two], tiles[one])
            out.append(kept + turn(moved, -step))
        tiles = out
    return tiles[0]


def swap_blocks(tiles):
    block = lane_block()
    out = []
    for g in range(4):
        acc = turn(tiles[0], -g)
        for b in range(1, 4):
            acc = jnp.where(block == b, turn(tiles[b], b - g), acc)
        out.append(acc)
    return out


def spread_blocks(tile):
    block = lane_block()
    turned = [turn(tile, k) for k in range(4)]
    out = []
    for b in range(4):
        acc = turned[(0 - b) % 4]
        for lane in range(1, 4):
            acc = jnp.where(block == lane, turned[(lane - b) % 4], acc)
        out.append(acc)
    return out


def kernel(
    grad_hbm,
    input_hbm,
    decay_hbm,
    freq_hbm,
    in_hbm,
    out_hbm,
    skip_hbm,
    docs,
    pieces,
    ret_ref,
    gb_ref,
    grad_v,
    input_v,
    param_v,
    skip_v,
    send_a,
    recv_a,
    coef,
    proj,
    skips,
    state,
    total,
    gd,
    ud,
    partial,
    send_d,
    recv_d,
    rows_d,
    pick,
    send_y,
    g_dp,
    g_all,
    load_sem,
    a_send,
    a_recv,
    d_send,
    d_recv,
    y_send,
    y_recv,
    p_send,
    p_recv,
    s_send,
    s_recv,
    c_send,
    c_recv,
):
    me = lax.axis_index("seq")
    core = lax.rem(me, 2)
    chip = me // 2
    row = lax.axis_index("dp")
    block = lane_block()
    own_block = lax.rem(me, 4)

    loads = []

    def load(src, dst):
        copy = pltpu.make_async_copy(src, dst, load_sem.at[len(loads)])
        copy.start()
        loads.append(copy)

    for c in range(SETS):
        wide = pl.ds(c * WIDE, WIDE)
        load(grad_hbm.at[0, :, wide], grad_v.at[c])
        load(input_hbm.at[0, :, wide], input_v.at[c])
    for c in range(SETS):
        tile = pl.ds(pl.multiple_of((4 * c + me // 4) * LANES, LANES), LANES)
        load(decay_hbm.at[:, tile], param_v.at[c, 0])
        load(freq_hbm.at[:, tile], param_v.at[c, 1])
        load(in_hbm.at[:, :, tile], param_v.at[c, pl.ds(2, 2)])
        load(out_hbm.at[:, :, tile], param_v.at[c, pl.ds(4, 2)])
        load(skip_hbm.at[:, tile], skip_v.at[c])

    barrier = pltpu.get_barrier_semaphore()

    def greet(k, _):
        pl.semaphore_signal(
            barrier, inc=1, device_id={"seq": lax.rem(me + k, SEQ)}, device_id_type=MESH
        )
        return 0

    lax.fori_loop(1, SEQ, greet, 0)
    for k in range(1, DP):
        pl.semaphore_signal(
            barrier, inc=1, device_id={"dp": lax.rem(row + k, DP)}, device_id_type=MESH
        )

    def copy_a(c, there, slot):
        return pltpu.make_async_remote_copy(
            src_ref=send_a.at[c, there],
            dst_ref=recv_a.at[c, slot],
            send_sem=a_send.at[c, there],
            recv_sem=a_recv.at[c, slot],
            device_id={"seq": there},
            device_id_type=MESH,
        )

    def pack(c):
        loads[2 * c].wait()
        loads[2 * c + 1].wait()
        for t in range(4):
            cols = slice(t * LANES, (t + 1) * LANES)
            for k, source in enumerate((grad_v, input_v)):
                tiles = interleave(source[c, :, cols].astype(F32))
                for g, tile in enumerate(swap_blocks(tiles)):
                    send_a[c, 4 * t + g, k * QUARTER : (k + 1) * QUARTER, :] = tile.astype(BF16)

    def launch(c):
        def one(k, _):
            copy_a(c, lax.rem(me + k, SEQ), me).start()
            return 0

        lax.fori_loop(1, SEQ, one, 0)
        recv_a[c, me] = send_a[c, me]

    pack(0)
    pl.semaphore_wait(barrier, SEQ - 1 + DP - 1)
    launch(0)
    pack(1)

    for copy in loads[2 * SETS :]:
        copy.wait()

    def own(tile, rows):
        acc = pltpu.roll(tile[:rows], lax.rem(4 - own_block, 4) * GROUP, 1)
        for q in range(1, 4):
            part = tile[:rows] if rows == 1 else tile[q * rows : (q + 1) * rows]
            turned = pltpu.roll(part, lax.rem(4 + q - own_block, 4) * GROUP, 1)
            acc = jnp.where(block == q, turned, acc)
        return acc

    for c in range(SETS):
        decay, freq, b_re, b_im, c_re, c_im = [own(param_v[c, k], ROWS) for k in range(6)]
        size = jnp.exp(-(decay / (SEQ * LEN)))
        coef[c, 0, 0] = size * jnp.cos(freq)
        coef[c, 0, 1] = -(size * jnp.sin(freq))
        coef[c, 1] = jnp.zeros((2, ROWS, LANES), F32)
        proj[c, 0] = b_re * c_re + b_im * c_im
        proj[c, 1] = b_im * c_re - b_re * c_im
        proj[c, 2] = c_re
        proj[c, 3] = c_im
        skips[c] = own(skip_v[c], 1)

    first = I32(0)
    slot = lax.broadcasted_iota(I32, (64, LEN), 0)
    place = lax.broadcasted_iota(I32, (64, LEN), 1)
    for j in range(DP):
        length = pieces[0, 0, j]
        chosen = (place - slot == first) & (slot < length)
        pick[j * 64 : (j + 1) * 64, :] = jnp.where(chosen, 1.0, 0.0).astype(BF16)
        first = first + length

    starts = [docs[0, 0]]
    for k in range(1, 3):
        starts.append(starts[-1] + docs[0, k])

    def copy_d(c, there, slot):
        return pltpu.make_async_remote_copy(
            src_ref=send_d.at[c, there],
            dst_ref=recv_d.at[c, slot],
            send_sem=d_send.at[c, there],
            recv_sem=d_recv.at[c, slot],
            device_id={"seq": there},
            device_id_type=MESH,
        )

    def send_home(c, t):
        @pl.when(t != me)
        def _():
            copy_d(c, t, me).start()

    def scan_segment(c, t):
        @pl.when(t != me)
        def _():
            copy_a(c, t, t).wait_recv()

        for k, dest in enumerate((gd, ud)):
            tile = recv_a[c, t, k * QUARTER : (k + 1) * QUARTER, :].astype(F32)
            for b, spread in enumerate(spread_blocks(tile)):
                for r in range(4):
                    at = 32 * r + 8 * b
                    dest[at : at + 8, :] = spread[8 * r : 8 * r + 8]

        x, y, sx, sy = state[0], state[1], total[0], total[1]
        sums = []
        for i in range(LEN - 1, -1, -1):
            after = t * LEN + (i + 1)
            cut = (after == starts[0]) | (after == starts[1]) | (after == starts[2])
            cut = cut.astype(I32)
            a_re = coef[c, cut, 0]
            a_im = coef[c, cut, 1]
            g = gd[i : i + 1, :]
            u = ud[i : i + 1, :]
            x, y = a_re * x + (g - a_im * y), a_re * y + a_im * x
            sx = sx + u * x
            sy = sy + u * y
            d = proj[c, 0] * x + proj[c, 1] * y
            sums.insert(0, d[:8] + d[8:])
            if i % 8 == 0:
                partial[i : i + 8, :] = fold_rows(sums)
                sums = []
        state[0], state[1], total[0], total[1] = x, y, sx, sy

        message = fold_blocks(interleave(partial[...]))
        message = message + skips[c] * recv_a[c, t, :QUARTER, :].astype(F32)
        message = message.astype(BF16)

        @pl.when(t != me)
        def _():
            send_d[c, t] = message

        @pl.when(t == me)
        def _():
            recv_d[c, me] = message

    def copy_y(c, there, slot):
        cols = pl.ds(pl.multiple_of(c * WIDE, WIDE), WIDE)
        return pltpu.make_async_remote_copy(
            src_ref=send_y.at[c, there],
            dst_ref=ret_ref.at[slot, :, cols],
            send_sem=y_send.at[c, there],
            recv_sem=y_recv.at[c, slot],
            device_id={"dp": there},
            device_id_type=MESH,
        )

    def deliver(c):
        def arrived(k, _):
            other = lax.rem(me + k, SEQ)
            copy_d(c, other, other).wait_recv()
            return 0

        lax.fori_loop(1, SEQ, arrived, 0)
        for t in range(4):
            tiles = [recv_d[c, 4 * t + g].astype(F32) for g in range(4)]
            tiles = swap_blocks(tiles)
            whole = [tiles[b][8 * r : 8 * r + 8] for r in range(4) for b in range(4)]
            whole = jnp.concatenate(whole, axis=0)
            rows_d[:, t * LANES : (t + 1) * LANES] = whole.astype(BF16)
        for j in range(DP):
            sent = jnp.dot(
                pick[j * 64 : (j + 1) * 64, :], rows_d[...], preferred_element_type=F32
            ).astype(BF16)
            send_y[c, j] = sent
        for k in range(1, DP):
            copy_y(c, lax.rem(row + k, DP), row).start()
        cols = pl.ds(pl.multiple_of(c * WIDE, WIDE), WIDE)
        ret_ref[row, :, cols] = send_y[c, row]

    def copy_p(c, there, slot):
        return pltpu.make_async_remote_copy(
            src_ref=g_dp.at[c, row],
            dst_ref=g_dp.at[c, slot],
            send_sem=p_send.at[c, there],
            recv_sem=p_recv.at[c, slot],
            device_id={"dp": there},
            device_id_type=MESH,
        )

    def copy_s(c, there, slot):
        return pltpu.make_async_remote_copy(
            src_ref=g_all.at[c, core, chip],
            dst_ref=g_all.at[c, core, slot],
            send_sem=s_send.at[c, there],
            recv_sem=s_recv.at[c, slot],
            device_id={"seq": 2 * there + core},
            device_id_type=MESH,
        )

    def copy_c(c, half):
        return pltpu.make_async_remote_copy(
            src_ref=g_all.at[c, half],
            dst_ref=g_all.at[c, half],
            send_sem=c_send.at[c],
            recv_sem=c_recv.at[c],
            device_id={"seq": 2 * chip + 1 - core},
            device_id_type=MESH,
        )

    def sum_own(c):
        sx, sy = total[0], total[1]
        c_re, c_im = proj[c, 2], proj[c, 3]
        g_dp[c, row, 0] = c_re * sx - c_im * sy
        g_dp[c, row, 1] = c_re * sy + c_im * sx
        for k in range(1, DP):
            copy_p(c, lax.rem(row + k, DP), row).start()

    def sum_rows(c):
        for k in range(1, DP):
            other = lax.rem(row + k, DP)
            copy_p(c, other, other).wait_recv()
        scale = math.sqrt(MODES / (DP * SEQ * LEN))
        g_all[c, core, chip] = ((g_dp[c, 0] + g_dp[c, 1]) + (g_dp[c, 2] + g_dp[c, 3])) * scale
        for k in range(1, HALF):
            copy_s(c, lax.rem(chip + k, HALF), chip).start()

    def to_sibling(c):
        for k in range(1, HALF):
            other = lax.rem(chip + k, HALF)
            copy_s(c, other, other).wait_recv()
        copy_c(c, core).start()

    def write_sums(c):
        copy_c(c, 1 - core).wait_recv()
        for t in range(4):
            cols = slice(c * WIDE + t * LANES, c * WIDE + (t + 1) * LANES)
            for k in range(2):
                tiles = [g_all[c, g % 2, 2 * t + g // 2, k] for g in range(4)]
                for q, tile in enumerate(swap_blocks(tiles)):
                    gb_ref[k, q * ROWS : (q + 1) * ROWS, cols] = tile

    def step(n, _):
        c = n // SEQ
        t = SEQ - 1 - lax.rem(n, SEQ)

        @pl.when(n == SECOND)
        def _():
            launch(1)

        @pl.when(n == SEQ)
        def _():
            sum_own(0)

        @pl.when(n == SEQ + 4)
        def _():
            sum_rows(0)

        last = n - SEQ

        @pl.when((last >= 0) & (last < HALF))
        def _():
            send_home(0, lax.rem(me + 2 * last + 1, SEQ))
            send_home(0, lax.rem(me + 2 * last + 2, SEQ))

        @pl.when(t == SEQ - 1)
        def _():
            state[...] = jnp.zeros_like(state)
            total[...] = jnp.zeros_like(total)

        scan_segment(c, t)

        @pl.when((last >= HALF - 1) & (last < HALF + 3))
        def _():
            for k in range(2):
                send_home(1, HALF + lax.rem(me + 2 * (last + 1) + k, HALF))

        @pl.when((last >= HALF + 3) & (last < HALF + 5))
        def _():
            for k in range(2):
                send_home(1, HALF // 2 + lax.rem(me + 2 * (last + 1) + k, HALF // 2))

        @pl.when(last == HALF + 5)
        def _():
            for k in range(2):
                send_home(1, 2 + lax.rem(me + k, 2))

        @pl.when(last >= HALF + 6)
        def _():
            send_home(1, t)

        @pl.when(last == SEQ - 3)
        def _():
            deliver(0)

        @pl.when((last == SEQ - 2) & (me >= HALF))
        def _():
            deliver(1)

        return 0

    lax.fori_loop(0, SETS * SEQ, step, 0)
    sum_own(1)
    to_sibling(0)
    sum_rows(1)

    @pl.when(me < HALF)
    def _():
        deliver(1)

    to_sibling(1)
    write_sums(0)
    write_sums(1)

    for c in range(SETS):
        for k in range(1, DP):
            other = lax.rem(row + k, DP)
            copy_y(c, other, other).wait_recv()
            copy_y(c, other, row).wait_send()
            copy_p(c, other, row).wait_send()
        for k in range(1, HALF):
            copy_s(c, lax.rem(chip + k, HALF), chip).wait_send()
        copy_c(c, core).wait_send()

        def left(k, _):
            other = lax.rem(me + k, SEQ)
            copy_a(c, other, me).wait_send()
            copy_d(c, other, me).wait_send()
            return 0

        lax.fori_loop(1, SEQ, left, 0)


def place_kernel(ret_in, gb_in, ret_out, gb_out, sem):
    copies = [
        pltpu.make_async_copy(ret_in.at[k], ret_out.at[k], sem.at[k]) for k in range(DP)
    ] + [pltpu.make_async_copy(gb_in.at[k], gb_out.at[k], sem.at[DP + k]) for k in range(2)]
    for copy in copies:
        copy.start()
    for copy in copies:
        copy.wait()


def shards(
    grad_out,
    inputs,
    decay_rate,
    frequency,
    in_proj,
    out_proj,
    skip_gain,
    doc_lengths,
    piece_lengths,
):
    anywhere = pl.BlockSpec(memory_space=pl.ANY)
    scalars = pl.BlockSpec(memory_space=pltpu.SMEM)
    vmem = pl.BlockSpec(memory_space=pltpu.VMEM)
    dma = pltpu.SemaphoreType.DMA
    returned, grad_b = pl.pallas_call(
        kernel,
        out_shape=(
            jax.ShapeDtypeStruct((DP, 64, SETS * WIDE), BF16),
            jax.ShapeDtypeStruct((2, MODES, SETS * WIDE), F32),
        ),
        in_specs=[anywhere] * 7 + [scalars] * 2,
        out_specs=(vmem, vmem),
        scratch_shapes=[
            pltpu.VMEM((SETS, LEN, WIDE), BF16),
            pltpu.VMEM((SETS, LEN, WIDE), BF16),
            pltpu.VMEM((SETS, 6, MODES, LANES), F32),
            pltpu.VMEM((SETS, 1, LANES), F32),
            pltpu.VMEM((SETS, SEQ, 2 * QUARTER, LANES), BF16),
            pltpu.VMEM((SETS, SEQ, 2 * QUARTER, LANES), BF16),
            pltpu.VMEM((SETS, 2, 2, ROWS, LANES), F32),
            pltpu.VMEM((SETS, 4, ROWS, LANES), F32),
            pltpu.VMEM((SETS, 1, LANES), F32),
            pltpu.VMEM((2, ROWS, LANES), F32),
            pltpu.VMEM((2, ROWS, LANES), F32),
            pltpu.VMEM((LEN, LANES), F32),
            pltpu.VMEM((LEN, LANES), F32),
            pltpu.VMEM((LEN, LANES), F32),
            pltpu.VMEM((SETS, SEQ, QUARTER, LANES), BF16),
            pltpu.VMEM((SETS, SEQ, QUARTER, LANES), BF16),
            pltpu.VMEM((LEN, WIDE), BF16),
            pltpu.VMEM((DP * 64, LEN), BF16),
            pltpu.VMEM((SETS, DP, 64, WIDE), BF16),
            pltpu.VMEM((SETS, DP, 2, ROWS, LANES), F32),
            pltpu.VMEM((SETS, 2, HALF, 2, ROWS, LANES), F32),
            dma((7 * SETS,)),
            dma((SETS, SEQ)),
            dma((SETS, SEQ)),
            dma((SETS, SEQ)),
            dma((SETS, SEQ)),
            dma((SETS, DP)),
            dma((SETS, DP)),
            dma((SETS, DP)),
            dma((SETS, DP)),
            dma((SETS, HALF)),
            dma((SETS, HALF)),
            dma((SETS,)),
            dma((SETS,)),
        ],
        compiler_params=pltpu.CompilerParams(
            collective_id=0, has_side_effects=True, vmem_limit_bytes=62 << 20
        ),
        cost_estimate=pl.CostEstimate(
            flops=15 * 128 * 64 * 1024, bytes_accessed=4 << 20, transcendentals=0
        ),
        name="scan_rows",
    )(
        grad_out,
        inputs,
        decay_rate,
        frequency,
        in_proj,
        out_proj,
        skip_gain[None],
        doc_lengths,
        piece_lengths,
    )
    returned, grad_b = pl.pallas_call(
        place_kernel,
        out_shape=(
            jax.ShapeDtypeStruct(returned.shape, BF16),
            jax.ShapeDtypeStruct(grad_b.shape, F32),
        ),
        in_specs=[vmem] * 2,
        out_specs=(anywhere, anywhere),
        scratch_shapes=[dma((DP + 2,))],
        compiler_params=pltpu.CompilerParams(vmem_limit_bytes=62 << 20),
        name="place_results",
    )(returned, grad_b)
    return returned[None, None], grad_b


def solution(mesh):
    return jax.shard_map(
        shards,
        mesh=mesh,
        in_specs=(
            P("dp", "seq", "ch"),
            P("dp", "seq", "ch"),
            P(None, "ch"),
            P(None, "ch"),
            P(None, None, "ch"),
            P(None, None, "ch"),
            P("ch"),
            P("dp", None),
            P("dp", "seq", None),
        ),
        out_specs=(P("seq", "dp", None, None, "ch"), P(None, None, "ch")),
        check_vma=False,
    )
```

```python
import math

import jax
import jax.numpy as jnp
from jax import lax
from jax.experimental import pallas as pl
from jax.experimental.pallas import tpu as pltpu
from jax.sharding import PartitionSpec as P

MESH = pl.DeviceIdType.MESH
F32 = jnp.float32
BF16 = jnp.bfloat16
I32 = jnp.int32

SEQ = 16
DP = 4
SETS = 2
LEN = 128
WIDE = 512
LANES = 128
GROUP = 32
QUARTER = 32
MODES = 64
ROWS = 16
HALF = SEQ // 2
EARLY = 4
SECOND = 4


def lane_block():
    return lax.broadcasted_iota(I32, (1, LANES), 1) // GROUP


def turn(tile, blocks):
    shift = (blocks % 4) * GROUP
    return tile if shift == 0 else pltpu.roll(tile, shift, 1)


def interleave(tile):
    return [
        jnp.concatenate([tile[32 * r + 8 * b : 32 * r + 8 * b + 8] for r in range(4)], axis=0)
        for b in range(4)
    ]


def fold_rows(tiles):
    place = lax.broadcasted_iota(I32, (8, 1), 0)
    for step in (1, 2, 4):
        first = (place & step) == 0
        out = []
        half = len(tiles) // 2
        pairs = [(2 * k, 2 * k + 1) for k in range(half)]
        for one, two in pairs:
            kept = jnp.where(first, tiles[one], tiles[two])
            moved = jnp.where(first, tiles[two], tiles[one])
            out.append(kept + pltpu.roll(moved, 8 - step, 0))
        tiles = out
    return tiles[0]


def fold_blocks(tiles):
    block = lane_block()
    for step in (1, 2):
        first = (block & step) == 0
        out = []
        for one, two in [(2 * k, 2 * k + 1) for k in range(len(tiles) // 2)]:
            kept = jnp.where(first, tiles[one], tiles[two])
            moved = jnp.where(first, tiles[two], tiles[one])
            out.append(kept + turn(moved, -step))
        tiles = out
    return tiles[0]


def swap_blocks(tiles):
    block = lane_block()
    out = []
    for g in range(4):
        acc = turn(tiles[0], -g)
        for b in range(1, 4):
            acc = jnp.where(block == b, turn(tiles[b], b - g), acc)
        out.append(acc)
    return out


def spread_blocks(tile):
    block = lane_block()
    turned = [turn(tile, k) for k in range(4)]
    out = []
    for b in range(4):
        acc = turned[(0 - b) % 4]
        for lane in range(1, 4):
            acc = jnp.where(block == lane, turned[(lane - b) % 4], acc)
        out.append(acc)
    return out


def kernel(
    grad_hbm,
    input_hbm,
    decay_hbm,
    freq_hbm,
    in_hbm,
    out_hbm,
    skip_hbm,
    docs,
    pieces,
    ret_ref,
    gb_ref,
    grad_v,
    input_v,
    param_v,
    skip_v,
    send_a,
    recv_a,
    coef,
    proj,
    skips,
    state,
    total,
    gd,
    ud,
    partial,
    send_d,
    recv_d,
    rows_d,
    pick,
    send_y,
    g_dp,
    g_all,
    load_sem,
    a_send,
    a_recv,
    d_send,
    d_recv,
    y_send,
    y_recv,
    p_send,
    p_recv,
    s_send,
    s_recv,
    c_send,
    c_recv,
):
    me = lax.axis_index("seq")
    core = lax.rem(me, 2)
    chip = me // 2
    row = lax.axis_index("dp")
    block = lane_block()
    own_block = lax.rem(me, 4)

    loads = []

    def load(src, dst):
        copy = pltpu.make_async_copy(src, dst, load_sem.at[len(loads)])
        copy.start()
        loads.append(copy)

    for c in range(SETS):
        wide = pl.ds(c * WIDE, WIDE)
        load(grad_hbm.at[0, :, wide], grad_v.at[c])
        load(input_hbm.at[0, :, wide], input_v.at[c])
    for c in range(SETS):
        tile = pl.ds(pl.multiple_of((4 * c + me // 4) * LANES, LANES), LANES)
        load(decay_hbm.at[:, tile], param_v.at[c, 0])
        load(freq_hbm.at[:, tile], param_v.at[c, 1])
        load(in_hbm.at[:, :, tile], param_v.at[c, pl.ds(2, 2)])
        load(out_hbm.at[:, :, tile], param_v.at[c, pl.ds(4, 2)])
        load(skip_hbm.at[:, tile], skip_v.at[c])

    barrier = pltpu.get_barrier_semaphore()

    def greet(k, _):
        pl.semaphore_signal(
            barrier, inc=1, device_id={"seq": lax.rem(me + k, SEQ)}, device_id_type=MESH
        )
        return 0

    lax.fori_loop(1, SEQ, greet, 0)
    for k in range(1, DP):
        pl.semaphore_signal(
            barrier, inc=1, device_id={"dp": lax.rem(row + k, DP)}, device_id_type=MESH
        )

    def copy_a(c, there, slot):
        return pltpu.make_async_remote_copy(
            src_ref=send_a.at[c, there],
            dst_ref=recv_a.at[c, slot],
            send_sem=a_send.at[c, there],
            recv_sem=a_recv.at[c, slot],
            device_id={"seq": there},
            device_id_type=MESH,
        )

    def pack(c):
        loads[2 * c].wait()
        loads[2 * c + 1].wait()
        for t in range(4):
            cols = slice(t * LANES, (t + 1) * LANES)
            for k, source in enumerate((grad_v, input_v)):
                tiles = interleave(source[c, :, cols].astype(F32))
                for g, tile in enumerate(swap_blocks(tiles)):
                    send_a[c, 4 * t + g, k * QUARTER : (k + 1) * QUARTER, :] = tile.astype(BF16)

    def launch(c):
        def one(k, _):
            copy_a(c, lax.rem(me + k, SEQ), me).start()
            return 0

        lax.fori_loop(1, SEQ, one, 0)
        recv_a[c, me] = send_a[c, me]

    pack(0)
    pl.semaphore_wait(barrier, SEQ - 1 + DP - 1)
    @pl.when(me >= EARLY)
    def _():
        launch(0)

    pack(1)

    for copy in loads[2 * SETS :]:
        copy.wait()

    def own(tile, rows):
        acc = pltpu.roll(tile[:rows], lax.rem(4 - own_block, 4) * GROUP, 1)
        for q in range(1, 4):
            part = tile[:rows] if rows == 1 else tile[q * rows : (q + 1) * rows]
            turned = pltpu.roll(part, lax.rem(4 + q - own_block, 4) * GROUP, 1)
            acc = jnp.where(block == q, turned, acc)
        return acc

    for c in range(SETS):
        decay, freq, b_re, b_im, c_re, c_im = [own(param_v[c, k], ROWS) for k in range(6)]
        size = jnp.exp(-(decay / (SEQ * LEN)))
        coef[c, 0, 0] = size * jnp.cos(freq)
        coef[c, 0, 1] = -(size * jnp.sin(freq))
        coef[c, 1] = jnp.zeros((2, ROWS, LANES), F32)
        proj[c, 0] = b_re * c_re + b_im * c_im
        proj[c, 1] = b_im * c_re - b_re * c_im
        proj[c, 2] = c_re
        proj[c, 3] = c_im
        skips[c] = own(skip_v[c], 1)

    first = I32(0)
    slot = lax.broadcasted_iota(I32, (64, LEN), 0)
    place = lax.broadcasted_iota(I32, (64, LEN), 1)
    for j in range(DP):
        length = pieces[0, 0, j]
        chosen = (place - slot == first) & (slot < length)
        pick[j * 64 : (j + 1) * 64, :] = jnp.where(chosen, 1.0, 0.0).astype(BF16)
        first = first + length

    starts = [docs[0, 0]]
    for k in range(1, 3):
        starts.append(starts[-1] + docs[0, k])

    def copy_d(c, there, slot):
        return pltpu.make_async_remote_copy(
            src_ref=send_d.at[c, there],
            dst_ref=recv_d.at[c, slot],
            send_sem=d_send.at[c, there],
            recv_sem=d_recv.at[c, slot],
            device_id={"seq": there},
            device_id_type=MESH,
        )

    def send_home(c, t):
        @pl.when(t != me)
        def _():
            copy_d(c, t, me).start()

    def scan_segment(c, t):
        @pl.when(t != me)
        def _():
            copy_a(c, t, t).wait_recv()

        first = c * SEQ + SEQ - 1 - t

        @pl.when((first == 0) & (me < EARLY))
        def _():
            launch(0)

        @pl.when(first == SECOND)
        def _():
            launch(1)

        for k, dest in enumerate((gd, ud)):
            tile = recv_a[c, t, k * QUARTER : (k + 1) * QUARTER, :].astype(F32)
            for b, spread in enumerate(spread_blocks(tile)):
                for r in range(4):
                    at = 32 * r + 8 * b
                    dest[at : at + 8, :] = spread[8 * r : 8 * r + 8]

        x, y, sx, sy = state[0], state[1], total[0], total[1]
        sums = []
        for i in range(LEN - 1, -1, -1):
            after = t * LEN + (i + 1)
            cut = (after == starts[0]) | (after == starts[1]) | (after == starts[2])
            cut = cut.astype(I32)
            a_re = coef[c, cut, 0]
            a_im = coef[c, cut, 1]
            g = gd[i : i + 1, :]
            u = ud[i : i + 1, :]
            x, y = a_re * x + (g - a_im * y), a_re * y + a_im * x
            sx = sx + u * x
            sy = sy + u * y
            d = proj[c, 0] * x + proj[c, 1] * y
            sums.insert(0, d[:8] + d[8:])
            if i % 8 == 0:
                partial[i : i + 8, :] = fold_rows(sums)
                sums = []
        state[0], state[1], total[0], total[1] = x, y, sx, sy

        message = fold_blocks(interleave(partial[...]))
        message = message + skips[c] * recv_a[c, t, :QUARTER, :].astype(F32)
        message = message.astype(BF16)

        @pl.when(t != me)
        def _():
            send_d[c, t] = message

        @pl.when(t == me)
        def _():
            recv_d[c, me] = message

    def copy_y(c, there, slot):
        cols = pl.ds(pl.multiple_of(c * WIDE, WIDE), WIDE)
        return pltpu.make_async_remote_copy(
            src_ref=send_y.at[c, there],
            dst_ref=ret_ref.at[slot, :, cols],
            send_sem=y_send.at[c, there],
            recv_sem=y_recv.at[c, slot],
            device_id={"dp": there},
            device_id_type=MESH,
        )

    def deliver(c):
        def arrived(k, _):
            other = lax.rem(me + k, SEQ)
            copy_d(c, other, other).wait_recv()
            return 0

        lax.fori_loop(1, SEQ, arrived, 0)
        for t in range(4):
            tiles = [recv_d[c, 4 * t + g].astype(F32) for g in range(4)]
            tiles = swap_blocks(tiles)
            whole = [tiles[b][8 * r : 8 * r + 8] for r in range(4) for b in range(4)]
            whole = jnp.concatenate(whole, axis=0)
            rows_d[:, t * LANES : (t + 1) * LANES] = whole.astype(BF16)
        for j in range(DP):
            sent = jnp.dot(
                pick[j * 64 : (j + 1) * 64, :], rows_d[...], preferred_element_type=F32
            ).astype(BF16)
            send_y[c, j] = sent
        for k in range(1, DP):
            copy_y(c, lax.rem(row + k, DP), row).start()
        cols = pl.ds(pl.multiple_of(c * WIDE, WIDE), WIDE)
        ret_ref[row, :, cols] = send_y[c, row]

    def copy_p(c, there, slot):
        return pltpu.make_async_remote_copy(
            src_ref=g_dp.at[c, row],
            dst_ref=g_dp.at[c, slot],
            send_sem=p_send.at[c, there],
            recv_sem=p_recv.at[c, slot],
            device_id={"dp": there},
            device_id_type=MESH,
        )

    def copy_s(c, there, slot):
        return pltpu.make_async_remote_copy(
            src_ref=g_all.at[c, core, chip],
            dst_ref=g_all.at[c, core, slot],
            send_sem=s_send.at[c, there],
            recv_sem=s_recv.at[c, slot],
            device_id={"seq": 2 * there + core},
            device_id_type=MESH,
        )

    def copy_c(c, half):
        return pltpu.make_async_remote_copy(
            src_ref=g_all.at[c, half],
            dst_ref=g_all.at[c, half],
            send_sem=c_send.at[c],
            recv_sem=c_recv.at[c],
            device_id={"seq": 2 * chip + 1 - core},
            device_id_type=MESH,
        )

    def sum_own(c):
        sx, sy = total[0], total[1]
        c_re, c_im = proj[c, 2], proj[c, 3]
        g_dp[c, row, 0] = c_re * sx - c_im * sy
        g_dp[c, row, 1] = c_re * sy + c_im * sx
        for k in range(1, DP):
            copy_p(c, lax.rem(row + k, DP), row).start()

    def sum_rows(c):
        for k in range(1, DP):
            other = lax.rem(row + k, DP)
            copy_p(c, other, other).wait_recv()
        scale = math.sqrt(MODES / (DP * SEQ * LEN))
        g_all[c, core, chip] = ((g_dp[c, 0] + g_dp[c, 1]) + (g_dp[c, 2] + g_dp[c, 3])) * scale
        for k in range(1, HALF):
            copy_s(c, lax.rem(chip + k, HALF), chip).start()

    def to_sibling(c):
        for k in range(1, HALF):
            other = lax.rem(chip + k, HALF)
            copy_s(c, other, other).wait_recv()
        copy_c(c, core).start()

    def write_sums(c):
        copy_c(c, 1 - core).wait_recv()
        for t in range(4):
            cols = slice(c * WIDE + t * LANES, c * WIDE + (t + 1) * LANES)
            for k in range(2):
                tiles = [g_all[c, g % 2, 2 * t + g // 2, k] for g in range(4)]
                for q, tile in enumerate(swap_blocks(tiles)):
                    gb_ref[k, q * ROWS : (q + 1) * ROWS, cols] = tile

    def step(n, _):
        c = n // SEQ
        t = SEQ - 1 - lax.rem(n, SEQ)

        @pl.when(n == SEQ)
        def _():
            sum_own(0)

        @pl.when(n == SEQ + 4)
        def _():
            sum_rows(0)

        last = n - SEQ

        @pl.when((last >= 0) & (last < HALF))
        def _():
            send_home(0, lax.rem(me + 2 * last + 1, SEQ))
            send_home(0, lax.rem(me + 2 * last + 2, SEQ))

        @pl.when(t == SEQ - 1)
        def _():
            state[...] = jnp.zeros_like(state)
            total[...] = jnp.zeros_like(total)

        scan_segment(c, t)

        @pl.when((last >= HALF - 1) & (last < HALF + 3))
        def _():
            for k in range(2):
                send_home(1, HALF + lax.rem(me + 2 * (last + 1) + k, HALF))

        @pl.when((last >= HALF + 3) & (last < HALF + 5))
        def _():
            for k in range(2):
                send_home(1, HALF // 2 + lax.rem(me + 2 * (last + 1) + k, HALF // 2))

        @pl.when(last == HALF + 5)
        def _():
            for k in range(2):
                send_home(1, 2 + lax.rem(me + k, 2))

        @pl.when(last >= HALF + 6)
        def _():
            send_home(1, t)

        @pl.when(last == SEQ - 3)
        def _():
            deliver(0)

        return 0

    lax.fori_loop(0, SETS * SEQ, step, 0)
    sum_own(1)
    to_sibling(0)
    sum_rows(1)

    deliver(1)

    to_sibling(1)
    write_sums(0)
    write_sums(1)

    for c in range(SETS):
        for k in range(1, DP):
            other = lax.rem(row + k, DP)
            copy_y(c, other, other).wait_recv()
            copy_y(c, other, row).wait_send()
            copy_p(c, other, row).wait_send()
        for k in range(1, HALF):
            copy_s(c, lax.rem(chip + k, HALF), chip).wait_send()
        copy_c(c, core).wait_send()

        def left(k, _):
            other = lax.rem(me + k, SEQ)
            copy_a(c, other, me).wait_send()
            copy_d(c, other, me).wait_send()
            return 0

        lax.fori_loop(1, SEQ, left, 0)


def place_kernel(ret_in, gb_in, ret_out, gb_out, sem):
    copies = [
        pltpu.make_async_copy(ret_in.at[k], ret_out.at[k], sem.at[k]) for k in range(DP)
    ] + [pltpu.make_async_copy(gb_in.at[k], gb_out.at[k], sem.at[DP + k]) for k in range(2)]
    for copy in copies:
        copy.start()
    for copy in copies:
        copy.wait()


def shards(
    grad_out,
    inputs,
    decay_rate,
    frequency,
    in_proj,
    out_proj,
    skip_gain,
    doc_lengths,
    piece_lengths,
):
    anywhere = pl.BlockSpec(memory_space=pl.ANY)
    scalars = pl.BlockSpec(memory_space=pltpu.SMEM)
    vmem = pl.BlockSpec(memory_space=pltpu.VMEM)
    dma = pltpu.SemaphoreType.DMA
    returned, grad_b = pl.pallas_call(
        kernel,
        out_shape=(
            jax.ShapeDtypeStruct((DP, 64, SETS * WIDE), BF16),
            jax.ShapeDtypeStruct((2, MODES, SETS * WIDE), F32),
        ),
        in_specs=[anywhere] * 7 + [scalars] * 2,
        out_specs=(vmem, vmem),
        scratch_shapes=[
            pltpu.VMEM((SETS, LEN, WIDE), BF16),
            pltpu.VMEM((SETS, LEN, WIDE), BF16),
            pltpu.VMEM((SETS, 6, MODES, LANES), F32),
            pltpu.VMEM((SETS, 1, LANES), F32),
            pltpu.VMEM((SETS, SEQ, 2 * QUARTER, LANES), BF16),
            pltpu.VMEM((SETS, SEQ, 2 * QUARTER, LANES), BF16),
            pltpu.VMEM((SETS, 2, 2, ROWS, LANES), F32),
            pltpu.VMEM((SETS, 4, ROWS, LANES), F32),
            pltpu.VMEM((SETS, 1, LANES), F32),
            pltpu.VMEM((2, ROWS, LANES), F32),
            pltpu.VMEM((2, ROWS, LANES), F32),
            pltpu.VMEM((LEN, LANES), F32),
            pltpu.VMEM((LEN, LANES), F32),
            pltpu.VMEM((LEN, LANES), F32),
            pltpu.VMEM((SETS, SEQ, QUARTER, LANES), BF16),
            pltpu.VMEM((SETS, SEQ, QUARTER, LANES), BF16),
            pltpu.VMEM((LEN, WIDE), BF16),
            pltpu.VMEM((DP * 64, LEN), BF16),
            pltpu.VMEM((SETS, DP, 64, WIDE), BF16),
            pltpu.VMEM((SETS, DP, 2, ROWS, LANES), F32),
            pltpu.VMEM((SETS, 2, HALF, 2, ROWS, LANES), F32),
            dma((7 * SETS,)),
            dma((SETS, SEQ)),
            dma((SETS, SEQ)),
            dma((SETS, SEQ)),
            dma((SETS, SEQ)),
            dma((SETS, DP)),
            dma((SETS, DP)),
            dma((SETS, DP)),
            dma((SETS, DP)),
            dma((SETS, HALF)),
            dma((SETS, HALF)),
            dma((SETS,)),
            dma((SETS,)),
        ],
        compiler_params=pltpu.CompilerParams(
            collective_id=0, has_side_effects=True, vmem_limit_bytes=62 << 20
        ),
        cost_estimate=pl.CostEstimate(
            flops=15 * 128 * 64 * 1024, bytes_accessed=4 << 20, transcendentals=0
        ),
        name="scan_rows",
    )(
        grad_out,
        inputs,
        decay_rate,
        frequency,
        in_proj,
        out_proj,
        skip_gain[None],
        doc_lengths,
        piece_lengths,
    )
    returned, grad_b = pl.pallas_call(
        place_kernel,
        out_shape=(
            jax.ShapeDtypeStruct(returned.shape, BF16),
            jax.ShapeDtypeStruct(grad_b.shape, F32),
        ),
        in_specs=[vmem] * 2,
        out_specs=(anywhere, anywhere),
        scratch_shapes=[dma((DP + 2,))],
        compiler_params=pltpu.CompilerParams(vmem_limit_bytes=62 << 20),
        name="place_results",
    )(returned, grad_b)
    return returned[None, None], grad_b


def solution(mesh):
    return jax.shard_map(
        shards,
        mesh=mesh,
        in_specs=(
            P("dp", "seq", "ch"),
            P("dp", "seq", "ch"),
            P(None, "ch"),
            P(None, "ch"),
            P(None, None, "ch"),
            P(None, None, "ch"),
            P("ch"),
            P("dp", None),
            P("dp", "seq", None),
        ),
        out_specs=(P("seq", "dp", None, None, "ch"), P(None, None, "ch")),
        check_vma=False,
    )
```

```python
import math

import jax
import jax.numpy as jnp
from jax import lax
from jax.experimental import pallas as pl
from jax.experimental.pallas import tpu as pltpu
from jax.sharding import PartitionSpec as P

MESH = pl.DeviceIdType.MESH
F32 = jnp.float32
BF16 = jnp.bfloat16
I32 = jnp.int32

SEQ = 16
DP = 4
SETS = 2
LEN = 128
WIDE = 512
LANES = 128
GROUP = 32
QUARTER = 32
MODES = 64
ROWS = 16
HALF = SEQ // 2
EARLY = 4
SECOND = 4


def lane_block():
    return lax.broadcasted_iota(I32, (1, LANES), 1) // GROUP


def turn(tile, blocks):
    shift = (blocks % 4) * GROUP
    return tile if shift == 0 else pltpu.roll(tile, shift, 1)


def interleave(tile):
    return [
        jnp.concatenate([tile[32 * r + 8 * b : 32 * r + 8 * b + 8] for r in range(4)], axis=0)
        for b in range(4)
    ]


def fold_rows(tiles):
    place = lax.broadcasted_iota(I32, (8, 1), 0)
    for step in (1, 2, 4):
        first = (place & step) == 0
        out = []
        half = len(tiles) // 2
        pairs = [(2 * k, 2 * k + 1) for k in range(half)]
        for one, two in pairs:
            kept = jnp.where(first, tiles[one], tiles[two])
            moved = jnp.where(first, tiles[two], tiles[one])
            out.append(kept + pltpu.roll(moved, 8 - step, 0))
        tiles = out
    return tiles[0]


def fold_blocks(tiles):
    block = lane_block()
    for step in (1, 2):
        first = (block & step) == 0
        out = []
        for one, two in [(2 * k, 2 * k + 1) for k in range(len(tiles) // 2)]:
            kept = jnp.where(first, tiles[one], tiles[two])
            moved = jnp.where(first, tiles[two], tiles[one])
            out.append(kept + turn(moved, -step))
        tiles = out
    return tiles[0]


def swap_blocks(tiles):
    block = lane_block()
    out = []
    for g in range(4):
        acc = turn(tiles[0], -g)
        for b in range(1, 4):
            acc = jnp.where(block == b, turn(tiles[b], b - g), acc)
        out.append(acc)
    return out


def spread_blocks(tile):
    block = lane_block()
    turned = [turn(tile, k) for k in range(4)]
    out = []
    for b in range(4):
        acc = turned[(0 - b) % 4]
        for lane in range(1, 4):
            acc = jnp.where(block == lane, turned[(lane - b) % 4], acc)
        out.append(acc)
    return out


def kernel(
    grad_hbm,
    input_hbm,
    decay_hbm,
    freq_hbm,
    in_hbm,
    out_hbm,
    skip_hbm,
    docs,
    pieces,
    ret_ref,
    gb_ref,
    grad_v,
    input_v,
    param_v,
    skip_v,
    send_a,
    recv_a,
    coef,
    proj,
    skips,
    state,
    total,
    gd,
    ud,
    partial,
    send_d,
    recv_d,
    rows_d,
    pick,
    send_y,
    g_dp,
    g_all,
    load_sem,
    a_send,
    a_recv,
    d_send,
    d_recv,
    y_send,
    y_recv,
    p_send,
    p_recv,
    s_send,
    s_recv,
    c_send,
    c_recv,
):
    me = lax.axis_index("seq")
    core = lax.rem(me, 2)
    chip = me // 2
    row = lax.axis_index("dp")
    block = lane_block()
    own_block = lax.rem(me, 4)

    loads = []

    def load(src, dst):
        copy = pltpu.make_async_copy(src, dst, load_sem.at[len(loads)])
        copy.start()
        loads.append(copy)

    for c in range(SETS):
        wide = pl.ds(c * WIDE, WIDE)
        load(grad_hbm.at[0, :, wide], grad_v.at[c])
        load(input_hbm.at[0, :, wide], input_v.at[c])
    for c in range(SETS):
        tile = pl.ds(pl.multiple_of((4 * c + me // 4) * LANES, LANES), LANES)
        load(decay_hbm.at[:, tile], param_v.at[c, 0])
        load(freq_hbm.at[:, tile], param_v.at[c, 1])
        load(in_hbm.at[:, :, tile], param_v.at[c, pl.ds(2, 2)])
        load(out_hbm.at[:, :, tile], param_v.at[c, pl.ds(4, 2)])
        load(skip_hbm.at[:, tile], skip_v.at[c])

    barrier = pltpu.get_barrier_semaphore()

    def greet(k, _):
        pl.semaphore_signal(
            barrier, inc=1, device_id={"seq": lax.rem(me + k, SEQ)}, device_id_type=MESH
        )
        return 0

    lax.fori_loop(1, SEQ, greet, 0)
    for k in range(1, DP):
        pl.semaphore_signal(
            barrier, inc=1, device_id={"dp": lax.rem(row + k, DP)}, device_id_type=MESH
        )

    def copy_a(c, there, slot):
        return pltpu.make_async_remote_copy(
            src_ref=send_a.at[c, there],
            dst_ref=recv_a.at[c, slot],
            send_sem=a_send.at[c, there],
            recv_sem=a_recv.at[c, slot],
            device_id={"seq": there},
            device_id_type=MESH,
        )

    def pack(c):
        loads[2 * c].wait()
        loads[2 * c + 1].wait()
        for t in range(4):
            cols = slice(t * LANES, (t + 1) * LANES)
            for k, source in enumerate((grad_v, input_v)):
                tiles = interleave(source[c, :, cols].astype(F32))
                for g, tile in enumerate(swap_blocks(tiles)):
                    send_a[c, 4 * t + g, k * QUARTER : (k + 1) * QUARTER, :] = tile.astype(BF16)

    def launch(c):
        def one(k, _):
            copy_a(c, lax.rem(me + k, SEQ), me).start()
            return 0

        lax.fori_loop(1, SEQ, one, 0)
        recv_a[c, me] = send_a[c, me]

    pack(0)
    pl.semaphore_wait(barrier, SEQ - 1 + DP - 1)
    @pl.when(me >= EARLY)
    def _():
        launch(0)

    pack(1)

    for copy in loads[2 * SETS :]:
        copy.wait()

    def own(tile, rows):
        acc = pltpu.roll(tile[:rows], lax.rem(4 - own_block, 4) * GROUP, 1)
        for q in range(1, 4):
            part = tile[:rows] if rows == 1 else tile[q * rows : (q + 1) * rows]
            turned = pltpu.roll(part, lax.rem(4 + q - own_block, 4) * GROUP, 1)
            acc = jnp.where(block == q, turned, acc)
        return acc

    for c in range(SETS):
        decay, freq, b_re, b_im, c_re, c_im = [own(param_v[c, k], ROWS) for k in range(6)]
        size = jnp.exp(-(decay / (SEQ * LEN)))
        coef[c, 0, 0] = size * jnp.cos(freq)
        coef[c, 0, 1] = -(size * jnp.sin(freq))
        coef[c, 1] = jnp.zeros((2, ROWS, LANES), F32)
        proj[c, 0] = b_re * c_re + b_im * c_im
        proj[c, 1] = b_im * c_re - b_re * c_im
        proj[c, 2] = c_re
        proj[c, 3] = c_im
        skips[c] = own(skip_v[c], 1)

    first = I32(0)
    slot = lax.broadcasted_iota(I32, (64, LEN), 0)
    place = lax.broadcasted_iota(I32, (64, LEN), 1)
    for j in range(DP):
        length = pieces[0, 0, j]
        chosen = (place - slot == first) & (slot < length)
        pick[j * 64 : (j + 1) * 64, :] = jnp.where(chosen, 1.0, 0.0).astype(BF16)
        first = first + length

    starts = [docs[0, 0]]
    for k in range(1, 3):
        starts.append(starts[-1] + docs[0, k])

    def copy_d(c, there, slot):
        return pltpu.make_async_remote_copy(
            src_ref=send_d.at[c, there],
            dst_ref=recv_d.at[c, slot],
            send_sem=d_send.at[c, there],
            recv_sem=d_recv.at[c, slot],
            device_id={"seq": there},
            device_id_type=MESH,
        )

    def send_home(c, t):
        @pl.when(t != me)
        def _():
            copy_d(c, t, me).start()

    def scan_segment(c, t):
        @pl.when(t != me)
        def _():
            copy_a(c, t, t).wait_recv()

        first = c * SEQ + SEQ - 1 - t

        @pl.when((first == 0) & (me < EARLY))
        def _():
            launch(0)

        @pl.when(first == SECOND)
        def _():
            launch(1)

        for k, dest in enumerate((gd, ud)):
            tile = recv_a[c, t, k * QUARTER : (k + 1) * QUARTER, :].astype(F32)
            for b, spread in enumerate(spread_blocks(tile)):
                for r in range(4):
                    at = 32 * r + 8 * b
                    dest[at : at + 8, :] = spread[8 * r : 8 * r + 8]

        x, y, sx, sy = state[0], state[1], total[0], total[1]
        sums = []
        for i in range(LEN - 1, -1, -1):
            after = t * LEN + (i + 1)
            cut = (after == starts[0]) | (after == starts[1]) | (after == starts[2])
            cut = cut.astype(I32)
            a_re = coef[c, cut, 0]
            a_im = coef[c, cut, 1]
            g = gd[i : i + 1, :]
            u = ud[i : i + 1, :]
            x, y = a_re * x + (g - a_im * y), a_re * y + a_im * x
            sx = sx + u * x
            sy = sy + u * y
            d = proj[c, 0] * x + proj[c, 1] * y
            sums.insert(0, d[:8] + d[8:])
            if i % 8 == 0:
                partial[i : i + 8, :] = fold_rows(sums)
                sums = []
        state[0], state[1], total[0], total[1] = x, y, sx, sy

        message = fold_blocks(interleave(partial[...]))
        message = message + skips[c] * recv_a[c, t, :QUARTER, :].astype(F32)
        message = message.astype(BF16)

        @pl.when(t != me)
        def _():
            send_d[c, t] = message

        @pl.when(t == me)
        def _():
            recv_d[c, me] = message

    def copy_y(c, there, slot):
        cols = pl.ds(pl.multiple_of(c * WIDE, WIDE), WIDE)
        return pltpu.make_async_remote_copy(
            src_ref=send_y.at[c, there],
            dst_ref=ret_ref.at[slot, :, cols],
            send_sem=y_send.at[c, there],
            recv_sem=y_recv.at[c, slot],
            device_id={"dp": there},
            device_id_type=MESH,
        )

    def deliver(c):
        def arrived(k, _):
            other = lax.rem(me + k, SEQ)
            copy_d(c, other, other).wait_recv()
            return 0

        lax.fori_loop(1, SEQ, arrived, 0)
        for t in range(4):
            tiles = [recv_d[c, 4 * t + g].astype(F32) for g in range(4)]
            tiles = swap_blocks(tiles)
            whole = [tiles[b][8 * r : 8 * r + 8] for r in range(4) for b in range(4)]
            whole = jnp.concatenate(whole, axis=0)
            rows_d[:, t * LANES : (t + 1) * LANES] = whole.astype(BF16)
        for j in range(DP):
            sent = jnp.dot(
                pick[j * 64 : (j + 1) * 64, :], rows_d[...], preferred_element_type=F32
            ).astype(BF16)
            send_y[c, j] = sent
        for k in range(1, DP):
            copy_y(c, lax.rem(row + k, DP), row).start()
        cols = pl.ds(pl.multiple_of(c * WIDE, WIDE), WIDE)
        ret_ref[row, :, cols] = send_y[c, row]

    def copy_p(c, there, slot):
        return pltpu.make_async_remote_copy(
            src_ref=g_dp.at[c, row],
            dst_ref=g_dp.at[c, slot],
            send_sem=p_send.at[c, there],
            recv_sem=p_recv.at[c, slot],
            device_id={"dp": there},
            device_id_type=MESH,
        )

    def copy_s(c, there, slot):
        return pltpu.make_async_remote_copy(
            src_ref=g_all.at[c, core, chip],
            dst_ref=g_all.at[c, core, slot],
            send_sem=s_send.at[c, there],
            recv_sem=s_recv.at[c, slot],
            device_id={"seq": 2 * there + core},
            device_id_type=MESH,
        )

    def copy_c(c, half):
        return pltpu.make_async_remote_copy(
            src_ref=g_all.at[c, half],
            dst_ref=g_all.at[c, half],
            send_sem=c_send.at[c],
            recv_sem=c_recv.at[c],
            device_id={"seq": 2 * chip + 1 - core},
            device_id_type=MESH,
        )

    def sum_own(c):
        sx, sy = total[0], total[1]
        c_re, c_im = proj[c, 2], proj[c, 3]
        g_dp[c, row, 0] = c_re * sx - c_im * sy
        g_dp[c, row, 1] = c_re * sy + c_im * sx
        for k in range(1, DP):
            copy_p(c, lax.rem(row + k, DP), row).start()

    def sum_rows(c):
        for k in range(1, DP):
            other = lax.rem(row + k, DP)
            copy_p(c, other, other).wait_recv()
        scale = math.sqrt(MODES / (DP * SEQ * LEN))
        g_all[c, core, chip] = ((g_dp[c, 0] + g_dp[c, 1]) + (g_dp[c, 2] + g_dp[c, 3])) * scale
        for k in range(1, HALF):
            copy_s(c, lax.rem(chip + k, HALF), chip).start()

    def to_sibling(c):
        for k in range(1, HALF):
            other = lax.rem(chip + k, HALF)
            copy_s(c, other, other).wait_recv()
        copy_c(c, core).start()

    def write_sums(c):
        copy_c(c, 1 - core).wait_recv()
        for t in range(4):
            cols = slice(c * WIDE + t * LANES, c * WIDE + (t + 1) * LANES)
            for k in range(2):
                tiles = [g_all[c, g % 2, 2 * t + g // 2, k] for g in range(4)]
                for q, tile in enumerate(swap_blocks(tiles)):
                    gb_ref[k, q * ROWS : (q + 1) * ROWS, cols] = tile

    def step(n, _):
        c = n // SEQ
        t = SEQ - 1 - lax.rem(n, SEQ)

        @pl.when(n == SEQ)
        def _():
            sum_own(0)

        @pl.when(n == SEQ + 9)
        def _():
            sum_rows(0)

        last = n - SEQ

        @pl.when((last >= 0) & (last < HALF))
        def _():
            send_home(0, lax.rem(me + 2 * last + 1, SEQ))
            send_home(0, lax.rem(me + 2 * last + 2, SEQ))

        @pl.when(t == SEQ - 1)
        def _():
            state[...] = jnp.zeros_like(state)
            total[...] = jnp.zeros_like(total)

        scan_segment(c, t)

        @pl.when((last >= HALF - 1) & (last < HALF + 3))
        def _():
            for k in range(2):
                send_home(1, HALF + lax.rem(me + 2 * (last + 1) + k, HALF))

        @pl.when((last >= HALF + 3) & (last < HALF + 5))
        def _():
            for k in range(2):
                send_home(1, HALF // 2 + lax.rem(me + 2 * (last + 1) + k, HALF // 2))

        @pl.when(last == HALF + 5)
        def _():
            for k in range(2):
                send_home(1, 2 + lax.rem(me + k, 2))

        @pl.when(last >= HALF + 6)
        def _():
            send_home(1, t)

        return 0

    lax.fori_loop(0, SETS * SEQ, step, 0)
    sum_own(1)
    deliver(0)
    to_sibling(0)
    sum_rows(1)

    deliver(1)

    to_sibling(1)
    write_sums(0)
    write_sums(1)

    for c in range(SETS):
        for k in range(1, DP):
            other = lax.rem(row + k, DP)
            copy_y(c, other, other).wait_recv()
            copy_y(c, other, row).wait_send()
            copy_p(c, other, row).wait_send()
        for k in range(1, HALF):
            copy_s(c, lax.rem(chip + k, HALF), chip).wait_send()
        copy_c(c, core).wait_send()

        def left(k, _):
            other = lax.rem(me + k, SEQ)
            copy_a(c, other, me).wait_send()
            copy_d(c, other, me).wait_send()
            return 0

        lax.fori_loop(1, SEQ, left, 0)


def place_kernel(ret_in, gb_in, ret_out, gb_out, sem):
    copies = [
        pltpu.make_async_copy(ret_in.at[k], ret_out.at[k], sem.at[k]) for k in range(DP)
    ] + [pltpu.make_async_copy(gb_in.at[k], gb_out.at[k], sem.at[DP + k]) for k in range(2)]
    for copy in copies:
        copy.start()
    for copy in copies:
        copy.wait()


def shards(
    grad_out,
    inputs,
    decay_rate,
    frequency,
    in_proj,
    out_proj,
    skip_gain,
    doc_lengths,
    piece_lengths,
):
    anywhere = pl.BlockSpec(memory_space=pl.ANY)
    scalars = pl.BlockSpec(memory_space=pltpu.SMEM)
    vmem = pl.BlockSpec(memory_space=pltpu.VMEM)
    dma = pltpu.SemaphoreType.DMA
    returned, grad_b = pl.pallas_call(
        kernel,
        out_shape=(
            jax.ShapeDtypeStruct((DP, 64, SETS * WIDE), BF16),
            jax.ShapeDtypeStruct((2, MODES, SETS * WIDE), F32),
        ),
        in_specs=[anywhere] * 7 + [scalars] * 2,
        out_specs=(vmem, vmem),
        scratch_shapes=[
            pltpu.VMEM((SETS, LEN, WIDE), BF16),
            pltpu.VMEM((SETS, LEN, WIDE), BF16),
            pltpu.VMEM((SETS, 6, MODES, LANES), F32),
            pltpu.VMEM((SETS, 1, LANES), F32),
            pltpu.VMEM((SETS, SEQ, 2 * QUARTER, LANES), BF16),
            pltpu.VMEM((SETS, SEQ, 2 * QUARTER, LANES), BF16),
            pltpu.VMEM((SETS, 2, 2, ROWS, LANES), F32),
            pltpu.VMEM((SETS, 4, ROWS, LANES), F32),
            pltpu.VMEM((SETS, 1, LANES), F32),
            pltpu.VMEM((2, ROWS, LANES), F32),
            pltpu.VMEM((2, ROWS, LANES), F32),
            pltpu.VMEM((LEN, LANES), F32),
            pltpu.VMEM((LEN, LANES), F32),
            pltpu.VMEM((LEN, LANES), F32),
            pltpu.VMEM((SETS, SEQ, QUARTER, LANES), BF16),
            pltpu.VMEM((SETS, SEQ, QUARTER, LANES), BF16),
            pltpu.VMEM((LEN, WIDE), BF16),
            pltpu.VMEM((DP * 64, LEN), BF16),
            pltpu.VMEM((SETS, DP, 64, WIDE), BF16),
            pltpu.VMEM((SETS, DP, 2, ROWS, LANES), F32),
            pltpu.VMEM((SETS, 2, HALF, 2, ROWS, LANES), F32),
            dma((7 * SETS,)),
            dma((SETS, SEQ)),
            dma((SETS, SEQ)),
            dma((SETS, SEQ)),
            dma((SETS, SEQ)),
            dma((SETS, DP)),
            dma((SETS, DP)),
            dma((SETS, DP)),
            dma((SETS, DP)),
            dma((SETS, HALF)),
            dma((SETS, HALF)),
            dma((SETS,)),
            dma((SETS,)),
        ],
        compiler_params=pltpu.CompilerParams(
            collective_id=0, has_side_effects=True, vmem_limit_bytes=62 << 20
        ),
        cost_estimate=pl.CostEstimate(
            flops=15 * 128 * 64 * 1024, bytes_accessed=4 << 20, transcendentals=0
        ),
        name="scan_rows",
    )(
        grad_out,
        inputs,
        decay_rate,
        frequency,
        in_proj,
        out_proj,
        skip_gain[None],
        doc_lengths,
        piece_lengths,
    )
    returned, grad_b = pl.pallas_call(
        place_kernel,
        out_shape=(
            jax.ShapeDtypeStruct(returned.shape, BF16),
            jax.ShapeDtypeStruct(grad_b.shape, F32),
        ),
        in_specs=[vmem] * 2,
        out_specs=(anywhere, anywhere),
        scratch_shapes=[dma((DP + 2,))],
        compiler_params=pltpu.CompilerParams(vmem_limit_bytes=62 << 20),
        name="place_results",
    )(returned, grad_b)
    return returned[None, None], grad_b


def solution(mesh):
    return jax.shard_map(
        shards,
        mesh=mesh,
        in_specs=(
            P("dp", "seq", "ch"),
            P("dp", "seq", "ch"),
            P(None, "ch"),
            P(None, "ch"),
            P(None, None, "ch"),
            P(None, None, "ch"),
            P("ch"),
            P("dp", None),
            P("dp", "seq", None),
        ),
        out_specs=(P("seq", "dp", None, None, "ch"), P(None, None, "ch")),
        check_vma=False,
    )
```

```python
import math

import jax
import jax.numpy as jnp
from jax import lax
from jax.experimental import pallas as pl
from jax.experimental.pallas import tpu as pltpu
from jax.sharding import PartitionSpec as P

MESH = pl.DeviceIdType.MESH
F32 = jnp.float32
BF16 = jnp.bfloat16
I32 = jnp.int32

SEQ = 16
DP = 4
SETS = 2
LEN = 128
WIDE = 512
LANES = 128
GROUP = 32
QUARTER = 32
MODES = 64
ROWS = 16
HALF = SEQ // 2
EARLY = 4
SECOND = 4


def lane_block():
    return lax.broadcasted_iota(I32, (1, LANES), 1) // GROUP


def turn(tile, blocks):
    shift = (blocks % 4) * GROUP
    return tile if shift == 0 else pltpu.roll(tile, shift, 1)


def interleave(tile):
    return [
        jnp.concatenate([tile[32 * r + 8 * b : 32 * r + 8 * b + 8] for r in range(4)], axis=0)
        for b in range(4)
    ]


def fold_rows(tiles):
    place = lax.broadcasted_iota(I32, (8, 1), 0)
    for step in (1, 2, 4):
        first = (place & step) == 0
        out = []
        half = len(tiles) // 2
        pairs = [(2 * k, 2 * k + 1) for k in range(half)]
        for one, two in pairs:
            kept = jnp.where(first, tiles[one], tiles[two])
            moved = jnp.where(first, tiles[two], tiles[one])
            out.append(kept + pltpu.roll(moved, 8 - step, 0))
        tiles = out
    return tiles[0]


def fold_blocks(tiles):
    block = lane_block()
    for step in (1, 2):
        first = (block & step) == 0
        out = []
        for one, two in [(2 * k, 2 * k + 1) for k in range(len(tiles) // 2)]:
            kept = jnp.where(first, tiles[one], tiles[two])
            moved = jnp.where(first, tiles[two], tiles[one])
            out.append(kept + turn(moved, -step))
        tiles = out
    return tiles[0]


def swap_blocks(tiles):
    block = lane_block()
    out = []
    for g in range(4):
        acc = turn(tiles[0], -g)
        for b in range(1, 4):
            acc = jnp.where(block == b, turn(tiles[b], b - g), acc)
        out.append(acc)
    return out


def spread_blocks(tile):
    block = lane_block()
    turned = [turn(tile, k) for k in range(4)]
    out = []
    for b in range(4):
        acc = turned[(0 - b) % 4]
        for lane in range(1, 4):
            acc = jnp.where(block == lane, turned[(lane - b) % 4], acc)
        out.append(acc)
    return out


def kernel(
    grad_hbm,
    input_hbm,
    decay_hbm,
    freq_hbm,
    in_hbm,
    out_hbm,
    skip_hbm,
    docs,
    pieces,
    ret_ref,
    gb_ref,
    grad_v,
    input_v,
    param_v,
    skip_v,
    send_a,
    recv_a,
    coef,
    proj,
    skips,
    state,
    total,
    gd,
    ud,
    partial,
    send_d,
    recv_d,
    rows_d,
    pick,
    send_y,
    g_dp,
    g_all,
    load_sem,
    a_send,
    a_recv,
    d_send,
    d_recv,
    y_send,
    y_recv,
    p_send,
    p_recv,
    s_send,
    s_recv,
    c_send,
    c_recv,
):
    me = lax.axis_index("seq")
    core = lax.rem(me, 2)
    chip = me // 2
    row = lax.axis_index("dp")
    block = lane_block()
    own_block = lax.rem(me, 4)

    loads = []

    def load(src, dst):
        copy = pltpu.make_async_copy(src, dst, load_sem.at[len(loads)])
        copy.start()
        loads.append(copy)

    for c in range(SETS):
        wide = pl.ds(c * WIDE, WIDE)
        load(grad_hbm.at[0, :, wide], grad_v.at[c])
        load(input_hbm.at[0, :, wide], input_v.at[c])
    for c in range(SETS):
        tile = pl.ds(pl.multiple_of((4 * c + me // 4) * LANES, LANES), LANES)
        load(decay_hbm.at[:, tile], param_v.at[c, 0])
        load(freq_hbm.at[:, tile], param_v.at[c, 1])
        load(in_hbm.at[:, :, tile], param_v.at[c, pl.ds(2, 2)])
        load(out_hbm.at[:, :, tile], param_v.at[c, pl.ds(4, 2)])
        load(skip_hbm.at[:, tile], skip_v.at[c])

    barrier = pltpu.get_barrier_semaphore()

    def greet(k, _):
        pl.semaphore_signal(
            barrier, inc=1, device_id={"seq": lax.rem(me + k, SEQ)}, device_id_type=MESH
        )
        return 0

    lax.fori_loop(1, SEQ, greet, 0)
    for k in range(1, DP):
        pl.semaphore_signal(
            barrier, inc=1, device_id={"dp": lax.rem(row + k, DP)}, device_id_type=MESH
        )

    def copy_a(c, there, slot):
        return pltpu.make_async_remote_copy(
            src_ref=send_a.at[c, there],
            dst_ref=recv_a.at[c, slot],
            send_sem=a_send.at[c, there],
            recv_sem=a_recv.at[c, slot],
            device_id={"seq": there},
            device_id_type=MESH,
        )

    def pack(c):
        loads[2 * c].wait()
        loads[2 * c + 1].wait()
        for t in range(4):
            cols = slice(t * LANES, (t + 1) * LANES)
            for k, source in enumerate((grad_v, input_v)):
                tiles = interleave(source[c, :, cols].astype(F32))
                for g, tile in enumerate(swap_blocks(tiles)):
                    send_a[c, 4 * t + g, k * QUARTER : (k + 1) * QUARTER, :] = tile.astype(BF16)

    def launch(c):
        def one(k, _):
            copy_a(c, lax.rem(me + k, SEQ), me).start()
            return 0

        lax.fori_loop(1, SEQ, one, 0)
        recv_a[c, me] = send_a[c, me]

    pack(0)
    pl.semaphore_wait(barrier, SEQ - 1 + DP - 1)
    @pl.when(me >= EARLY)
    def _():
        launch(0)

    pack(1)

    for copy in loads[2 * SETS :]:
        copy.wait()

    def own(tile, rows):
        acc = pltpu.roll(tile[:rows], lax.rem(4 - own_block, 4) * GROUP, 1)
        for q in range(1, 4):
            part = tile[:rows] if rows == 1 else tile[q * rows : (q + 1) * rows]
            turned = pltpu.roll(part, lax.rem(4 + q - own_block, 4) * GROUP, 1)
            acc = jnp.where(block == q, turned, acc)
        return acc

    for c in range(SETS):
        decay, freq, b_re, b_im, c_re, c_im = [own(param_v[c, k], ROWS) for k in range(6)]
        size = jnp.exp(-(decay / (SEQ * LEN)))
        coef[c, 0, 0] = size * jnp.cos(freq)
        coef[c, 0, 1] = -(size * jnp.sin(freq))
        coef[c, 1] = jnp.zeros((2, ROWS, LANES), F32)
        proj[c, 0] = b_re * c_re + b_im * c_im
        proj[c, 1] = b_im * c_re - b_re * c_im
        proj[c, 2] = c_re
        proj[c, 3] = c_im
        skips[c] = own(skip_v[c], 1)

    first = I32(0)
    slot = lax.broadcasted_iota(I32, (64, LEN), 0)
    place = lax.broadcasted_iota(I32, (64, LEN), 1)
    for j in range(DP):
        length = pieces[0, 0, j]
        chosen = (place - slot == first) & (slot < length)
        pick[j * 64 : (j + 1) * 64, :] = jnp.where(chosen, 1.0, 0.0).astype(BF16)
        first = first + length

    starts = [docs[0, 0]]
    for k in range(1, 3):
        starts.append(starts[-1] + docs[0, k])

    def copy_d(c, there, slot):
        return pltpu.make_async_remote_copy(
            src_ref=send_d.at[c, there],
            dst_ref=recv_d.at[c, slot],
            send_sem=d_send.at[c, there],
            recv_sem=d_recv.at[c, slot],
            device_id={"seq": there},
            device_id_type=MESH,
        )

    def send_home(c, t):
        @pl.when(t != me)
        def _():
            copy_d(c, t, me).start()

    def scan_segment(c, t):
        @pl.when(t != me)
        def _():
            copy_a(c, t, t).wait_recv()

        first = c * SEQ + SEQ - 1 - t

        @pl.when((first == 0) & (me < EARLY))
        def _():
            launch(0)

        @pl.when(first == SECOND)
        def _():
            launch(1)

        for k, dest in enumerate((gd, ud)):
            tile = recv_a[c, t, k * QUARTER : (k + 1) * QUARTER, :].astype(F32)
            for b, spread in enumerate(spread_blocks(tile)):
                for r in range(4):
                    at = 32 * r + 8 * b
                    dest[at : at + 8, :] = spread[8 * r : 8 * r + 8]

        x, y, sx, sy = state[0], state[1], total[0], total[1]
        sums = []
        for i in range(LEN - 1, -1, -1):
            after = t * LEN + (i + 1)
            cut = (after == starts[0]) | (after == starts[1]) | (after == starts[2])
            cut = cut.astype(I32)
            a_re = coef[c, cut, 0]
            a_im = coef[c, cut, 1]
            g = gd[i : i + 1, :]
            u = ud[i : i + 1, :]
            x, y = a_re * x + (g - a_im * y), a_re * y + a_im * x
            sx = sx + u * x
            sy = sy + u * y
            d = proj[c, 0] * x + proj[c, 1] * y
            sums.insert(0, d[:8] + d[8:])
            if i % 8 == 0:
                partial[i : i + 8, :] = fold_rows(sums)
                sums = []
        state[0], state[1], total[0], total[1] = x, y, sx, sy

        message = fold_blocks(interleave(partial[...]))
        message = message + skips[c] * recv_a[c, t, :QUARTER, :].astype(F32)
        message = message.astype(BF16)

        @pl.when(t != me)
        def _():
            send_d[c, t] = message

        @pl.when(t == me)
        def _():
            recv_d[c, me] = message

    def copy_y(c, there, slot):
        cols = pl.ds(pl.multiple_of(c * WIDE, WIDE), WIDE)
        return pltpu.make_async_remote_copy(
            src_ref=send_y.at[c, there],
            dst_ref=ret_ref.at[slot, :, cols],
            send_sem=y_send.at[c, there],
            recv_sem=y_recv.at[c, slot],
            device_id={"dp": there},
            device_id_type=MESH,
        )

    def deliver(c):
        def arrived(k, _):
            other = lax.rem(me + k, SEQ)
            copy_d(c, other, other).wait_recv()
            return 0

        lax.fori_loop(1, SEQ, arrived, 0)
        for t in range(4):
            tiles = [recv_d[c, 4 * t + g].astype(F32) for g in range(4)]
            tiles = swap_blocks(tiles)
            whole = [tiles[b][8 * r : 8 * r + 8] for r in range(4) for b in range(4)]
            whole = jnp.concatenate(whole, axis=0)
            rows_d[:, t * LANES : (t + 1) * LANES] = whole.astype(BF16)
        for j in range(DP):
            sent = jnp.dot(
                pick[j * 64 : (j + 1) * 64, :], rows_d[...], preferred_element_type=F32
            ).astype(BF16)
            send_y[c, j] = sent
        for k in range(1, DP):
            copy_y(c, lax.rem(row + k, DP), row).start()
        cols = pl.ds(pl.multiple_of(c * WIDE, WIDE), WIDE)
        ret_ref[row, :, cols] = send_y[c, row]

    def copy_p(c, there, slot):
        return pltpu.make_async_remote_copy(
            src_ref=g_dp.at[c, row],
            dst_ref=g_dp.at[c, slot],
            send_sem=p_send.at[c, there],
            recv_sem=p_recv.at[c, slot],
            device_id={"dp": there},
            device_id_type=MESH,
        )

    def copy_s(c, there, slot):
        return pltpu.make_async_remote_copy(
            src_ref=g_all.at[c, core, chip],
            dst_ref=g_all.at[c, core, slot],
            send_sem=s_send.at[c, there],
            recv_sem=s_recv.at[c, slot],
            device_id={"seq": 2 * there + core},
            device_id_type=MESH,
        )

    def copy_c(c, half):
        return pltpu.make_async_remote_copy(
            src_ref=g_all.at[c, half],
            dst_ref=g_all.at[c, half],
            send_sem=c_send.at[c],
            recv_sem=c_recv.at[c],
            device_id={"seq": 2 * chip + 1 - core},
            device_id_type=MESH,
        )

    def sum_own(c):
        sx, sy = total[0], total[1]
        c_re, c_im = proj[c, 2], proj[c, 3]
        g_dp[c, row, 0] = c_re * sx - c_im * sy
        g_dp[c, row, 1] = c_re * sy + c_im * sx
        for k in range(1, DP):
            copy_p(c, lax.rem(row + k, DP), row).start()

    def sum_rows(c):
        for k in range(1, DP):
            other = lax.rem(row + k, DP)
            copy_p(c, other, other).wait_recv()
        scale = math.sqrt(MODES / (DP * SEQ * LEN))
        g_all[c, core, chip] = ((g_dp[c, 0] + g_dp[c, 1]) + (g_dp[c, 2] + g_dp[c, 3])) * scale
        for k in range(1, HALF):
            copy_s(c, lax.rem(chip + k, HALF), chip).start()

    def to_sibling(c):
        for k in range(1, HALF):
            other = lax.rem(chip + k, HALF)
            copy_s(c, other, other).wait_recv()
        copy_c(c, core).start()

    def write_sums(c):
        copy_c(c, 1 - core).wait_recv()
        for t in range(4):
            cols = slice(c * WIDE + t * LANES, c * WIDE + (t + 1) * LANES)
            for k in range(2):
                tiles = [g_all[c, g % 2, 2 * t + g // 2, k] for g in range(4)]
                for q, tile in enumerate(swap_blocks(tiles)):
                    gb_ref[k, q * ROWS : (q + 1) * ROWS, cols] = tile

    def step(n, _):
        c = n // SEQ
        t = SEQ - 1 - lax.rem(n, SEQ)

        @pl.when(n == SEQ)
        def _():
            sum_own(0)

        @pl.when(n == SEQ + 9)
        def _():
            sum_rows(0)

        last = n - SEQ

        @pl.when((last >= 0) & (last < HALF))
        def _():
            send_home(0, lax.rem(me + 2 * last + 1, SEQ))
            send_home(0, lax.rem(me + 2 * last + 2, SEQ))

        @pl.when(t == SEQ - 1)
        def _():
            state[...] = jnp.zeros_like(state)
            total[...] = jnp.zeros_like(total)

        scan_segment(c, t)

        @pl.when((last >= HALF - 1) & (last < HALF + 3))
        def _():
            for k in range(2):
                send_home(1, HALF + lax.rem(me + 2 * (last + 1) + k, HALF))

        @pl.when((last >= HALF + 3) & (last < HALF + 5))
        def _():
            for k in range(2):
                send_home(1, HALF // 2 + lax.rem(me + 2 * (last + 1) + k, HALF // 2))

        @pl.when(last == HALF + 5)
        def _():
            for k in range(2):
                send_home(1, 2 + lax.rem(me + k, 2))

        @pl.when(last >= HALF + 6)
        def _():
            send_home(1, t)

        return 0

    lax.fori_loop(0, SETS * SEQ, step, 0)
    sum_own(1)
    deliver(0)
    sum_rows(1)
    to_sibling(0)

    deliver(1)

    to_sibling(1)
    write_sums(0)
    write_sums(1)

    for c in range(SETS):
        for k in range(1, DP):
            other = lax.rem(row + k, DP)
            copy_y(c, other, other).wait_recv()
            copy_y(c, other, row).wait_send()
            copy_p(c, other, row).wait_send()
        for k in range(1, HALF):
            copy_s(c, lax.rem(chip + k, HALF), chip).wait_send()
        copy_c(c, core).wait_send()

        def left(k, _):
            other = lax.rem(me + k, SEQ)
            copy_a(c, other, me).wait_send()
            copy_d(c, other, me).wait_send()
            return 0

        lax.fori_loop(1, SEQ, left, 0)


def place_kernel(ret_in, gb_in, ret_out, gb_out, sem):
    copies = [
        pltpu.make_async_copy(ret_in.at[k], ret_out.at[k], sem.at[k]) for k in range(DP)
    ] + [pltpu.make_async_copy(gb_in.at[k], gb_out.at[k], sem.at[DP + k]) for k in range(2)]
    for copy in copies:
        copy.start()
    for copy in copies:
        copy.wait()


def shards(
    grad_out,
    inputs,
    decay_rate,
    frequency,
    in_proj,
    out_proj,
    skip_gain,
    doc_lengths,
    piece_lengths,
):
    anywhere = pl.BlockSpec(memory_space=pl.ANY)
    scalars = pl.BlockSpec(memory_space=pltpu.SMEM)
    vmem = pl.BlockSpec(memory_space=pltpu.VMEM)
    dma = pltpu.SemaphoreType.DMA
    returned, grad_b = pl.pallas_call(
        kernel,
        out_shape=(
            jax.ShapeDtypeStruct((DP, 64, SETS * WIDE), BF16),
            jax.ShapeDtypeStruct((2, MODES, SETS * WIDE), F32),
        ),
        in_specs=[anywhere] * 7 + [scalars] * 2,
        out_specs=(vmem, vmem),
        scratch_shapes=[
            pltpu.VMEM((SETS, LEN, WIDE), BF16),
            pltpu.VMEM((SETS, LEN, WIDE), BF16),
            pltpu.VMEM((SETS, 6, MODES, LANES), F32),
            pltpu.VMEM((SETS, 1, LANES), F32),
            pltpu.VMEM((SETS, SEQ, 2 * QUARTER, LANES), BF16),
            pltpu.VMEM((SETS, SEQ, 2 * QUARTER, LANES), BF16),
            pltpu.VMEM((SETS, 2, 2, ROWS, LANES), F32),
            pltpu.VMEM((SETS, 4, ROWS, LANES), F32),
            pltpu.VMEM((SETS, 1, LANES), F32),
            pltpu.VMEM((2, ROWS, LANES), F32),
            pltpu.VMEM((2, ROWS, LANES), F32),
            pltpu.VMEM((LEN, LANES), F32),
            pltpu.VMEM((LEN, LANES), F32),
            pltpu.VMEM((LEN, LANES), F32),
            pltpu.VMEM((SETS, SEQ, QUARTER, LANES), BF16),
            pltpu.VMEM((SETS, SEQ, QUARTER, LANES), BF16),
            pltpu.VMEM((LEN, WIDE), BF16),
            pltpu.VMEM((DP * 64, LEN), BF16),
            pltpu.VMEM((SETS, DP, 64, WIDE), BF16),
            pltpu.VMEM((SETS, DP, 2, ROWS, LANES), F32),
            pltpu.VMEM((SETS, 2, HALF, 2, ROWS, LANES), F32),
            dma((7 * SETS,)),
            dma((SETS, SEQ)),
            dma((SETS, SEQ)),
            dma((SETS, SEQ)),
            dma((SETS, SEQ)),
            dma((SETS, DP)),
            dma((SETS, DP)),
            dma((SETS, DP)),
            dma((SETS, DP)),
            dma((SETS, HALF)),
            dma((SETS, HALF)),
            dma((SETS,)),
            dma((SETS,)),
        ],
        compiler_params=pltpu.CompilerParams(
            collective_id=0, has_side_effects=True, vmem_limit_bytes=62 << 20
        ),
        cost_estimate=pl.CostEstimate(
            flops=15 * 128 * 64 * 1024, bytes_accessed=4 << 20, transcendentals=0
        ),
        name="scan_rows",
    )(
        grad_out,
        inputs,
        decay_rate,
        frequency,
        in_proj,
        out_proj,
        skip_gain[None],
        doc_lengths,
        piece_lengths,
    )
    returned, grad_b = pl.pallas_call(
        place_kernel,
        out_shape=(
            jax.ShapeDtypeStruct(returned.shape, BF16),
            jax.ShapeDtypeStruct(grad_b.shape, F32),
        ),
        in_specs=[vmem] * 2,
        out_specs=(anywhere, anywhere),
        scratch_shapes=[dma((DP + 2,))],
        compiler_params=pltpu.CompilerParams(vmem_limit_bytes=62 << 20),
        name="place_results",
    )(returned, grad_b)
    return returned[None, None], grad_b


def solution(mesh):
    return jax.shard_map(
        shards,
        mesh=mesh,
        in_specs=(
            P("dp", "seq", "ch"),
            P("dp", "seq", "ch"),
            P(None, "ch"),
            P(None, "ch"),
            P(None, None, "ch"),
            P(None, None, "ch"),
            P("ch"),
            P("dp", None),
            P("dp", "seq", None),
        ),
        out_specs=(P("seq", "dp", None, None, "ch"), P(None, None, "ch")),
        check_vma=False,
    )
```
